512 devices in a mesh: rows: 128 (over y, z, core), cols: 4 (over x).
Axes of the slice: x: 4, y: 8, z: 8, core: 2. Of those that a mesh axis runs over, the one named last changes fastest.
Arguments:
- panel: float32 [16, 8388608], P('cols', 'rows')
- signs: int32 [8388608], P('rows'), may hold values from -1 to 1, as said below
- samples: int32 [65536], replicated, may hold values from 0 to 8388607, as said below
Outputs:
- factor: float32 [16, 16], replicated
- normalized: float32 [16, 114688], P('cols', 'rows')
The draws below stay inside these ranges and needn't reach their ends.
Inputs may be any that keep to these rules, and one draw needn't show every extreme that they name: samples is strictly increasing. For every block d of positions, at most 896 samples g have (g mod 65536) // 512 == d, and some block has exactly 896. `signs`: every entry is -1 or 1.
All inputs are finite; a program needn't handle non-finite values.
Results may differ from the reference program's by a relative error of at most 0.00016.
Values sent between devices are 32-bit elements; how exact they have to be, the bound alone decides.
A program may use at most 128 MiB of HBM per device.

```python
import math
import jax
import jax.numpy as jnp
from jax import lax

COLS = 16
R_DEV = 65536
SAMP_DEV = 512
CAP = 896
BLK = 512
TOTAL_ROWS = 8388608
SAMPLES = 65536
N_ROWS = 128


def draw_panel(key, part):
    key = jax.random.fold_in(key, 11)
    key_main, key_rows = jax.random.split(key, 2)
    column_scale = 10.0 ** ((jnp.arange(COLS, dtype=jnp.float32) - (COLS - 1)) / (COLS - 1))
    row_scale = jnp.exp(jax.random.uniform(key_rows, (TOTAL_ROWS,), jnp.float32, 0.0, math.log(10.0)))
    noise = jax.random.normal(key_main, (COLS, TOTAL_ROWS), jnp.float32)
    return (noise * column_scale[:, None] * row_scale[None, :]).astype(jnp.float32)


def draw_signs(key, part):
    key = jax.random.fold_in(key, 23)
    return 2 * jax.random.randint(key, (TOTAL_ROWS,), 0, 2, jnp.int32) - 1


def draw_samples(key, part):
    key = jax.random.fold_in(key, 37)
    key_count, key_force, key_pick = jax.random.split(key, 3)
    pairs = N_ROWS // 2
    first = jax.random.randint(key_count, (pairs,), SAMP_DEV // 4, CAP + 1, jnp.int32)
    forced = jax.random.randint(key_force, (), 0, pairs, jnp.int32)
    first = jnp.where(jnp.arange(pairs, dtype=jnp.int32) == forced, CAP, first)
    counts = jnp.stack([first, 2 * SAMP_DEV - first], axis=1).reshape(N_ROWS)
    block_keys = jax.random.split(key_pick, N_ROWS)
    ranks = jax.vmap(lambda single: jax.random.permutation(single, R_DEV))(block_keys)
    chosen = ranks < counts[:, None]
    chosen = chosen.reshape(N_ROWS, N_ROWS, BLK).transpose(1, 0, 2).reshape(TOTAL_ROWS)
    return jnp.nonzero(chosen, size=SAMPLES, fill_value=0)[0].astype(jnp.int32)


def setup_inputs(seed: int = 0) -> dict:
    keys = jax.random.split(jax.random.key(seed), 4)
    return {
        "panel": draw_panel(jax.random.fold_in(keys[3], 71), 0),
        "signs": draw_signs(jax.random.fold_in(keys[3], 71), 0),
        "samples": draw_samples(jax.random.fold_in(keys[3], 71), 0),
    }


def hadamard(order):
    first = jnp.arange(order, dtype=jnp.int32)
    both = jnp.bitwise_and(first[:, None], first[None, :])
    parity = jnp.zeros((order, order), jnp.int32)
    for level in range(max(order.bit_length() - 1, 0)):
        parity = parity + jnp.bitwise_and(jnp.right_shift(both, level), 1)
    parity = parity % 2
    return (1 - 2 * parity).astype(jnp.float32)

def reference(panel, signs, samples):
    total = TOTAL_ROWS
    bits = R_DEV.bit_length() - 1
    outer = 1 << bits // 2
    inner = R_DEV // outer
    values = panel * signs[None, :].astype(jnp.float32) * (1.0 / math.sqrt(total))
    values = values.reshape(COLS, N_ROWS, outer, inner)
    high = lax.Precision.HIGHEST
    values = jnp.einsum('cpab,jb->cpaj', values, hadamard(inner), precision=high)
    values = jnp.einsum('ia,cpaj->cpij', hadamard(outer), values, precision=high)
    values = jnp.einsum('qp,cpij->cqij', hadamard(N_ROWS), values, precision=high)
    mixed = values.reshape(COLS, total)
    picked = jnp.take(mixed, samples, axis=1)
    gram = jnp.dot(picked, picked.T, precision=high) / SAMPLES
    lower = jnp.linalg.cholesky(gram)
    solved = jax.scipy.linalg.solve_triangular(lower, picked, lower=True)
    owner = (samples % R_DEV // BLK).astype(jnp.int32)
    order = jnp.argsort(owner, stable=True).astype(jnp.int32)
    sorted_owner = owner[order]
    starts = jnp.searchsorted(sorted_owner, sorted_owner, side='left').astype(jnp.int32)
    ranks_sorted = jnp.arange(SAMPLES, dtype=jnp.int32) - starts
    ranks = jnp.zeros((SAMPLES,), jnp.int32).at[order].set(ranks_sorted)
    slot_index = owner * CAP + ranks
    normalized = jnp.zeros((COLS, N_ROWS * CAP), jnp.float32).at[:, slot_index].set(solved)
    return (lower.T, normalized)
```

```python
import math

import jax
import jax.numpy as jnp
from jax import lax
from jax.experimental import pallas as pl
from jax.experimental.pallas import tpu as pltpu
from jax.sharding import PartitionSpec as P

LINE = 8
BLK = 512
LANES = 128
SLOT_ROWS = 7
CAP = SLOT_ROWS * LANES
WIDTH = 4
ORDER = 256
SHARDS = 128
LOCAL = ORDER * ORDER
SAMPLE_ROWS = 512
COLS = 16
MESH = pl.DeviceIdType.MESH
HIGHEST = lax.Precision.HIGHEST
DISTANCES = (4, 3, 5, 2, 6, 1, 7)


def iota(shape, axis):
    return lax.broadcasted_iota(jnp.int32, shape, axis)


def parity(value):
    value = value ^ (value >> 4)
    value = value ^ (value >> 2)
    value = value ^ (value >> 1)
    return value & 1


def hadamard_rows(rows):
    odd = parity(rows & iota((ORDER, ORDER), 1))
    return (1 - 2 * odd).astype(jnp.float32).astype(jnp.bfloat16)


def line_rows(half):
    place = iota((ORDER, ORDER), 0)
    line, core, other, part = place >> 5, (place >> 4) & 1, (place >> 1) & 7, place & 1
    if half == 0:
        return other * 32 + line * 4 + core * 2 + part
    return line * 32 + other * 4 + core * 2 + part


def split(values):
    high = values.astype(jnp.bfloat16)
    low = (values - high.astype(jnp.float32)).astype(jnp.bfloat16)
    return high, low


def dot(a, b):
    return jnp.dot(a, b, preferred_element_type=jnp.float32)


def slot_list(samples, device):
    turned = jnp.transpose(samples)
    pieces = [turned & 255, (turned >> 8) & 255, turned >> 16]
    pieces = [p.astype(jnp.float32).astype(jnp.bfloat16) for p in pieces]
    last = samples[:, LANES - 1 :].astype(jnp.float32)
    lane = iota((1, 2 * SHARDS), 1)
    edge = (lane & (SHARDS - 1)) * LOCAL + device * BLK + (lane >> 7) * BLK
    edge = edge.astype(jnp.float32)
    before = jnp.sum((last < edge).astype(jnp.float32), axis=0, keepdims=True)
    row_id = iota((SAMPLE_ROWS, 1), 0).astype(jnp.float32)
    hot = (row_id == before).astype(jnp.float32).astype(jnp.bfloat16)
    rows = dot(jnp.concatenate(pieces, axis=0), hot)
    rows = rows[:LANES] + 256.0 * rows[LANES : 2 * LANES] + 65536.0 * rows[2 * LANES :]
    inside = jnp.sum((rows < edge).astype(jnp.float32), axis=0, keepdims=True)
    whole = jnp.float32(SAMPLE_ROWS * LANES)
    place = jnp.where(before >= SAMPLE_ROWS, whole, before * LANES + inside)
    first = place[:, :SHARDS]
    count = place[:, SHARDS:] - first
    square_row, square_col = iota((SHARDS, SHARDS), 0), iota((SHARDS, SHARDS), 1)
    first_col = jnp.sum(
        jnp.where(square_row == square_col, first, 0.0), axis=1, keepdims=True
    )
    start_col = jnp.sum(
        jnp.where(square_col < square_row, count, 0.0), axis=1, keepdims=True
    )
    end_col = jnp.sum(
        jnp.where(square_col <= square_row, count, 0.0), axis=1, keepdims=True
    )
    slot = iota((1, CAP), 1).astype(jnp.float32)
    owner = jnp.sum((slot >= end_col).astype(jnp.float32), axis=0, keepdims=True)
    shard_id = iota((SHARDS, 1), 0).astype(jnp.float32)
    shift = jnp.sum(
        jnp.where(shard_id == owner, first_col - start_col, 0.0), axis=0, keepdims=True
    )
    index = slot + shift
    row = jnp.floor(index * (1.0 / LANES))
    column = index - row * LANES
    hot = (row_id == row).astype(jnp.float32).astype(jnp.bfloat16)
    bit = ((turned >> 8) & 1).astype(jnp.float32).astype(jnp.bfloat16)
    found = dot(jnp.concatenate([pieces[0], bit], axis=0), hot)
    found = found[:LANES] + 256.0 * found[LANES:]
    lane_id = iota((LANES, 1), 0).astype(jnp.float32)
    position = jnp.sum(
        jnp.where(lane_id == column, found, 0.0), axis=0, keepdims=True
    )
    used = owner < SHARDS
    code = jnp.where(used, owner * BLK + position, 0.0)
    return code.astype(jnp.int32), used.astype(jnp.float32)


def kernel(
    panel,
    signs,
    samples,
    factor,
    normalized,
    panel_v,
    signs_v,
    samples_v,
    sent,
    got,
    own_list,
    own_used,
    lists,
    codes,
    sums,
    part_sent,
    part_got,
    picked,
    gram_one,
    gram_two,
    local_sem,
    sent_sem,
    got_sem,
    list_out_sem,
    list_in_sem,
    part_out_sem,
    part_in_sem,
    picked_out_sem,
    picked_in_sem,
    one_out_sem,
    one_in_sem,
    two_out_sem,
    two_in_sem,
):
    scale = 1.0 / math.sqrt(LOCAL * SHARDS)
    me = lax.axis_index("rows")
    my_col = lax.axis_index("cols")
    my_y, my_z, my_core = me >> 4, (me >> 1) & 7, me & 1
    my_lines = (my_z, my_y)

    def device(half, line, core):
        if half == 0:
            return (my_y * 16 + line * 2 + core, my_col)
        return (line * 16 + my_z * 2 + core, my_col)

    def on_line(half, distance):
        return (my_lines[half] + distance) & 7

    loads = [
        pltpu.make_async_copy(samples, samples_v, local_sem.at[0]),
        pltpu.make_async_copy(signs, signs_v, local_sem.at[1]),
        pltpu.make_async_copy(panel, panel_v, local_sem.at[2]),
    ]
    for load in loads:
        load.start()

    barrier = pltpu.get_barrier_semaphore()

    def greet(target):
        pl.semaphore_signal(barrier, inc=1, device_id=target, device_id_type=MESH)

    greet(device(0, my_z, 1 - my_core))
    for distance in DISTANCES:
        for half in range(2):
            for flip in range(2):
                greet(device(half, on_line(half, distance), my_core ^ flip))
    for step in range(1, 4):
        greet((me, (my_col + step) & 3))

    loads[0].wait()
    code, used = slot_list(samples_v[...], me)
    for t in range(SLOT_ROWS):
        own_list[t : t + 1, :] = code[:, t * LANES : (t + 1) * LANES]
        own_used[t : t + 1, :] = used[:, t * LANES : (t + 1) * LANES]
    own_list[SLOT_ROWS:, :] = jnp.zeros((1, LANES), jnp.int32)
    own_used[SLOT_ROWS:, :] = jnp.zeros((1, LANES), jnp.float32)

    inner = hadamard_rows(iota((ORDER, ORDER), 0))
    outer = []
    for half in range(2):
        matrix = hadamard_rows(line_rows(half))
        outer.append(jnp.concatenate([matrix, matrix], axis=1))

    loads[1].wait()
    loads[2].wait()
    pl.semaphore_wait(barrier, 32)

    list_copies = []
    for half in range(2):
        lists[half, my_lines[half]] = own_list[...]
        for distance in DISTANCES:
            line = on_line(half, distance)
            copy = pltpu.make_async_remote_copy(
                src_ref=own_list,
                dst_ref=lists.at[half, my_lines[half]],
                send_sem=list_out_sem.at[half, line],
                recv_sem=list_in_sem.at[half, my_lines[half]],
                device_id=device(half, line, my_core),
                device_id_type=MESH,
            )
            copy.start()
            list_copies.append(copy)

    flip_signs = jnp.concatenate(
        [signs_v[pl.ds(j, ORDER, stride=2), :] for j in range(2)], axis=1
    )
    flip_signs = flip_signs.astype(jnp.float32) * scale
    my_sources = [my_lines[half] * 2 + my_core for half in range(2)]

    def block_copy(half, column, line, core):
        target = line * 2 + core
        return pltpu.make_async_remote_copy(
            src_ref=sent.at[half, target, column],
            dst_ref=got.at[half, my_sources[half], column],
            send_sem=sent_sem.at[half, target, column],
            recv_sem=got_sem.at[half, my_sources[half], column],
            device_id=device(half, line, core),
            device_id_type=MESH,
        )

    for column in range(2):
        for half in range(2):
            which = half * 2 + column
            values = jnp.concatenate(
                [panel_v[pl.ds(4 * j + which, ORDER, stride=8), :] for j in range(2)],
                axis=1,
            )
            high, low = split(values * flip_signs)
            values = dot(jnp.concatenate([high, low], axis=0), inner)
            values = values[:ORDER] + values[ORDER:]
            high, low = split(values)
            values = dot(outer[half], jnp.concatenate([high, low], axis=0))
            sent[half, :, column] = values.reshape(16, 16, ORDER)
            for distance in DISTANCES:
                for flip in range(2):
                    block_copy(
                        half, column, on_line(half, distance), my_core ^ flip
                    ).start()
            block_copy(half, column, my_lines[half], 1 - my_core).start()

    spread = iota((8, LANES), 0) >> 1
    for half in range(2):
        for distance in DISTANCES:
            line = on_line(half, distance)
            pltpu.make_async_remote_copy(
                src_ref=own_list,
                dst_ref=lists.at[half, line],
                send_sem=list_out_sem.at[half, line],
                recv_sem=list_in_sem.at[half, line],
                device_id=device(half, line, my_core),
                device_id_type=MESH,
            ).wait_recv()
        flat = lists.at[half].reshape(64, LANES)
        for t in range(SLOT_ROWS):
            rows = flat[pl.ds(t, 8, stride=8), :]
            for group in range(2):
                codes[1 - half, group, t] = jnp.take_along_axis(
                    rows, spread + 4 * group, axis=0
                )

    odd_row = iota((8, LANES), 0) & 1

    def add_source(half, column, source, table, first):
        for group in range(2):
            left = table[group * 8 : group * 8 + 8, :LANES]
            right = table[group * 8 : group * 8 + 8, LANES:]
            for t in range(SLOT_ROWS):
                code = codes[half, group, t]
                lane = code & (LANES - 1)
                a = jnp.take_along_axis(left, lane, axis=1)
                b = jnp.take_along_axis(right, lane, axis=1)
                value = jnp.where((code & LANES) != 0, b, a)
                shard = code >> 9
                if half == 0:
                    bits = shard & source
                else:
                    bits = shard & ((source >> 1) * 16 + (source & 1))
                value = jnp.where(parity(bits) != 0, -value, value)
                if first:
                    sums[half, column, group, t] = value
                else:
                    sums[half, column, group, t] += value

    def part_copy(half, column, line):
        return pltpu.make_async_remote_copy(
            src_ref=part_sent.at[half, column, line],
            dst_ref=part_got.at[half, column, my_lines[half]],
            send_sem=part_out_sem.at[half, column, line],
            recv_sem=part_in_sem.at[half, column, my_lines[half]],
            device_id=device(half, line, my_core),
            device_id_type=MESH,
        )

    for column in range(2):
        for half in range(2):
            mine = my_sources[half]
            add_source(half, column, mine, sent.at[half, mine, column], True)

            def from_source(line, core, half=half, column=column):
                source = line * 2 + core
                pltpu.make_async_remote_copy(
                    src_ref=sent.at[half, source, column],
                    dst_ref=got.at[half, source, column],
                    send_sem=sent_sem.at[half, source, column],
                    recv_sem=got_sem.at[half, source, column],
                    device_id=device(half, line, core),
                    device_id_type=MESH,
                ).wait_recv()
                add_source(
                    half, column, source, got.at[half, source, column], False
                )

            from_source(my_lines[half], 1 - my_core)

            def body(step, carry, half=half, from_source=from_source):
                order = step >> 1
                away = (order + 1) >> 1
                distance = 4 + away * (1 - 2 * (order & 1))
                from_source(on_line(half, distance), my_core ^ (step & 1))
                return carry

            lax.fori_loop(0, 14, body, 0)

            other = 1 - half
            for group in range(2):
                for t in range(SLOT_ROWS):
                    code = codes[half, group, t]
                    value = sums[half, column, group, t]
                    value = jnp.where(((code >> 8) & 1) == odd_row, value, 0.0)
                    value = value + pltpu.roll(value, 7, 0)
                    for line in range(4):
                        part_sent[other, column, group * 4 + line, t : t + 1, :] = (
                            value[2 * line : 2 * line + 1]
                        )
            for line in range(8):
                part_sent[other, column, line, SLOT_ROWS:, :] = jnp.zeros(
                    (1, LANES), jnp.float32
                )
            for distance in DISTANCES:
                part_copy(other, column, on_line(other, distance)).start()

    own_code = own_list[...] >> 9
    own_mask = own_used[...]
    for column in range(2):
        for half in range(2):
            other = 1 - half
            line = my_lines[other]
            bits = own_code >> 1 if other == 0 else own_code >> 4

            def signed(line, value):
                return jnp.where(parity(bits & line & 7) != 0, -value, value)

            total = signed(line, part_sent[other, column, line])
            for distance in DISTANCES:
                line = on_line(other, distance)
                pltpu.make_async_remote_copy(
                    src_ref=part_sent.at[other, column, line],
                    dst_ref=part_got.at[other, column, line],
                    send_sem=part_out_sem.at[other, column, line],
                    recv_sem=part_in_sem.at[other, column, line],
                    device_id=device(other, line, my_core),
                    device_id_type=MESH,
                ).wait_recv()
                total += signed(line, part_got[other, column, line])
            which = half * 2 + column
            picked[my_col, which * 8 : which * 8 + 8, :] = total * own_mask

    for step in range(1, 4):
        pltpu.make_async_remote_copy(
            src_ref=picked.at[my_col],
            dst_ref=picked.at[my_col],
            send_sem=picked_out_sem.at[(my_col + step) & 3],
            recv_sem=picked_in_sem.at[my_col],
            device_id=(me, (my_col + step) & 3),
            device_id_type=MESH,
        ).start()
    for step in range(1, 4):
        source = (my_col + step) & 3
        pltpu.make_async_remote_copy(
            src_ref=picked.at[my_col],
            dst_ref=picked.at[source],
            send_sem=picked_out_sem.at[source],
            recv_sem=picked_in_sem.at[source],
            device_id=(me, source),
            device_id_type=MESH,
        ).wait_recv()
    flat = picked.reshape(COLS * 8, LANES)
    panel_rows = jnp.concatenate(
        [flat[pl.ds(t, COLS, stride=8), :] for t in range(SLOT_ROWS)], axis=1
    )

    wide = lax.dot_general(
        panel_rows,
        jnp.concatenate([panel_rows] * 8, axis=0),
        (((1,), (1,)), ((), ())),
        precision=HIGHEST,
        preferred_element_type=jnp.float32,
    )
    keep = (iota((COLS, LANES), 1) >> 4) == (iota((COLS, LANES), 0) & 7)
    wide = jnp.where(keep, wide, 0.0) * (1.0 / (SAMPLE_ROWS * LANES))
    mine = my_sources[0]
    gram_one[mine] = jnp.concatenate(
        [
            jnp.sum(wide[:8], axis=0, keepdims=True),
            jnp.sum(wide[8:], axis=0, keepdims=True),
        ],
        axis=0,
    )

    sources = [(my_z, 1 - my_core)]
    for distance in DISTANCES:
        for flip in range(2):
            sources.append((on_line(0, distance), my_core ^ flip))
    for line, core in sources:
        pltpu.make_async_remote_copy(
            src_ref=gram_one.at[mine],
            dst_ref=gram_one.at[mine],
            send_sem=one_out_sem.at[line * 2 + core],
            recv_sem=one_in_sem.at[mine],
            device_id=device(0, line, core),
            device_id_type=MESH,
        ).start()
    for line, core in sources:
        pltpu.make_async_remote_copy(
            src_ref=gram_one.at[mine],
            dst_ref=gram_one.at[line * 2 + core],
            send_sem=one_out_sem.at[line * 2 + core],
            recv_sem=one_in_sem.at[line * 2 + core],
            device_id=device(0, line, core),
            device_id_type=MESH,
        ).wait_recv()
    gram_two[my_y] = jnp.sum(gram_one[...], axis=0)
    for distance in DISTANCES:
        line = on_line(1, distance)
        pltpu.make_async_remote_copy(
            src_ref=gram_two.at[my_y],
            dst_ref=gram_two.at[my_y],
            send_sem=two_out_sem.at[line],
            recv_sem=two_in_sem.at[my_y],
            device_id=device(1, line, my_core),
            device_id_type=MESH,
        ).start()
    for distance in DISTANCES:
        line = on_line(1, distance)
        pltpu.make_async_remote_copy(
            src_ref=gram_two.at[my_y],
            dst_ref=gram_two.at[line],
            send_sem=two_out_sem.at[line],
            recv_sem=two_in_sem.at[line],
            device_id=device(1, line, my_core),
            device_id_type=MESH,
        ).wait_recv()
    gram = jnp.sum(gram_two[...], axis=0)

    row = iota((COLS, LANES), 0)
    lane = iota((COLS, LANES), 1)
    rows = jnp.concatenate(
        [jnp.broadcast_to(gram[i : i + 1], (8, LANES)) for i in range(2)], axis=0
    )
    rows = jnp.take_along_axis(rows, ((row & 7) * 16 + lane) & (LANES - 1), axis=1)
    unit = jnp.where(lane - COLS == row, 1.0, 0.0)
    both = jnp.where(lane < COLS, rows, unit)
    for j in range(COLS - 1):
        pivot_row = jnp.broadcast_to(both[j : j + 1], (COLS, LANES))
        pivot = jnp.take_along_axis(pivot_row, jnp.full_like(lane, j), axis=1)
        column = jnp.take_along_axis(both, jnp.full_like(lane, j), axis=1)
        column = jnp.where(row > j, column, 0.0)
        both = both - column * (pivot_row / pivot)
    pivots = jnp.take_along_axis(both, row, axis=1)
    both = both / jnp.sqrt(pivots)
    factor[...] = jnp.where(lane >= row, both, 0.0)[:, :COLS]

    pick_row = iota((8, COLS), 1) == iota((8, COLS), 0) + my_col * WIDTH
    own = jnp.dot(
        pick_row.astype(jnp.float32),
        both[:, COLS : 2 * COLS],
        precision=HIGHEST,
        preferred_element_type=jnp.float32,
    )
    own = jnp.dot(
        own, panel_rows, precision=HIGHEST, preferred_element_type=jnp.float32
    )
    normalized[...] = own[:WIDTH]

    for copy in list_copies:
        copy.wait_send()
    for column in range(2):
        for half in range(2):
            block_copy(half, column, my_lines[half], 1 - my_core).wait_send()
            for distance in DISTANCES:
                for flip in range(2):
                    block_copy(
                        half, column, on_line(half, distance), my_core ^ flip
                    ).wait_send()
                part_copy(half, column, on_line(half, distance)).wait_send()
    for step in range(1, 4):
        pltpu.make_async_remote_copy(
            src_ref=picked.at[my_col],
            dst_ref=picked.at[my_col],
            send_sem=picked_out_sem.at[(my_col + step) & 3],
            recv_sem=picked_in_sem.at[my_col],
            device_id=(me, (my_col + step) & 3),
            device_id_type=MESH,
        ).wait_send()
    for line, core in sources:
        pltpu.make_async_remote_copy(
            src_ref=gram_one.at[mine],
            dst_ref=gram_one.at[mine],
            send_sem=one_out_sem.at[line * 2 + core],
            recv_sem=one_in_sem.at[mine],
            device_id=device(0, line, core),
            device_id_type=MESH,
        ).wait_send()
    for distance in DISTANCES:
        line = on_line(1, distance)
        pltpu.make_async_remote_copy(
            src_ref=gram_two.at[my_y],
            dst_ref=gram_two.at[my_y],
            send_sem=two_out_sem.at[line],
            recv_sem=two_in_sem.at[my_y],
            device_id=device(1, line, my_core),
            device_id_type=MESH,
        ).wait_send()


def local(panel, signs, samples):
    panel = panel.reshape(WIDTH, 2 * ORDER, LANES).transpose(1, 0, 2)
    panel = panel.reshape(2 * ORDER * WIDTH, LANES)
    signs = signs.reshape(2 * ORDER, LANES)
    samples = samples.reshape(SAMPLE_ROWS, LANES)
    f32, i32, dma = jnp.float32, jnp.int32, pltpu.SemaphoreType.DMA
    factor, normalized = pl.pallas_call(
        kernel,
        out_shape=(
            jax.ShapeDtypeStruct((COLS, COLS), f32),
            jax.ShapeDtypeStruct((WIDTH, CAP), f32),
        ),
        in_specs=[pl.BlockSpec(memory_space=pl.ANY)] * 3,
        out_specs=[pl.BlockSpec(memory_space=pltpu.VMEM)] * 2,
        scratch_shapes=[
            pltpu.VMEM((2 * ORDER * WIDTH, LANES), f32),
            pltpu.VMEM((2 * ORDER, LANES), i32),
            pltpu.VMEM((SAMPLE_ROWS, LANES), i32),
            pltpu.VMEM((2, 16, 2, 16, ORDER), f32),
            pltpu.VMEM((2, 16, 2, 16, ORDER), f32),
            pltpu.VMEM((8, LANES), i32),
            pltpu.VMEM((8, LANES), f32),
            pltpu.VMEM((2, 8, 8, LANES), i32),
            pltpu.VMEM((2, 2, SLOT_ROWS, 8, LANES), i32),
            pltpu.VMEM((2, 2, 2, SLOT_ROWS, 8, LANES), f32),
            pltpu.VMEM((2, 2, 8, 8, LANES), f32),
            pltpu.VMEM((2, 2, 8, 8, LANES), f32),
            pltpu.VMEM((4, 8 * WIDTH, LANES), f32),
            pltpu.VMEM((16, 2, LANES), f32),
            pltpu.VMEM((8, 2, LANES), f32),
            dma((3,)),
            dma((2, 16, 2)),
            dma((2, 16, 2)),
            dma((2, 8)),
            dma((2, 8)),
            dma((2, 2, 8)),
            dma((2, 2, 8)),
            dma((4,)),
            dma((4,)),
            dma((16,)),
            dma((16,)),
            dma((8,)),
            dma((8,)),
        ],
        compiler_params=pltpu.CompilerParams(
            collective_id=0, has_side_effects=True, vmem_limit_bytes=32 * 1024 * 1024
        ),
    )(panel, signs, samples)
    return factor, normalized


def solution(mesh):
    return jax.shard_map(
        local,
        mesh=mesh,
        in_specs=(P("cols", "rows"), P("rows"), P()),
        out_specs=(P(), P("cols", "rows")),
        check_vma=False,
    )
```

```python
import math

import jax
import jax.numpy as jnp
from jax import lax
from jax.experimental import pallas as pl
from jax.experimental.pallas import tpu as pltpu
from jax.sharding import PartitionSpec as P

LINE = 8
BLK = 512
LANES = 128
SLOT_ROWS = 7
CAP = SLOT_ROWS * LANES
WIDTH = 4
ORDER = 256
SHARDS = 128
LOCAL = ORDER * ORDER
SAMPLE_ROWS = 512
COLS = 16
MESH = pl.DeviceIdType.MESH
HIGHEST = lax.Precision.HIGHEST
DISTANCES = (4, 3, 5, 2, 6, 1, 7)
OFFSETS = sorted(
    ((y, z, c) for y in range(8) for z in range(8) for c in range(2) if y or z or c),
    key=lambda at: -min(at[0], 8 - at[0]) - min(at[1], 8 - at[1]),
)


def iota(shape, axis):
    return lax.broadcasted_iota(jnp.int32, shape, axis)


def parity(value):
    value = value ^ (value >> 4)
    value = value ^ (value >> 2)
    value = value ^ (value >> 1)
    return value & 1


def hadamard_rows(rows):
    odd = parity(rows & iota((ORDER, ORDER), 1))
    return (1 - 2 * odd).astype(jnp.float32).astype(jnp.bfloat16)


def line_rows(half):
    place = iota((ORDER, ORDER), 0)
    line, core, other, part = place >> 5, (place >> 4) & 1, (place >> 1) & 7, place & 1
    if half == 0:
        return other * 32 + line * 4 + core * 2 + part
    return line * 32 + other * 4 + core * 2 + part


def split(values):
    high = values.astype(jnp.bfloat16)
    low = (values - high.astype(jnp.float32)).astype(jnp.bfloat16)
    return high, low


def dot(a, b):
    return jnp.dot(a, b, preferred_element_type=jnp.float32)


def slot_list(samples, device):
    turned = jnp.transpose(samples)
    pieces = [turned & 255, (turned >> 8) & 255, turned >> 16]
    pieces = [p.astype(jnp.float32).astype(jnp.bfloat16) for p in pieces]
    last = samples[:, LANES - 1 :].astype(jnp.float32)
    lane = iota((1, 2 * SHARDS), 1)
    edge = (lane & (SHARDS - 1)) * LOCAL + device * BLK + (lane >> 7) * BLK
    edge = edge.astype(jnp.float32)
    before = jnp.sum((last < edge).astype(jnp.float32), axis=0, keepdims=True)
    row_id = iota((SAMPLE_ROWS, 1), 0).astype(jnp.float32)
    hot = (row_id == before).astype(jnp.float32).astype(jnp.bfloat16)
    rows = dot(jnp.concatenate(pieces, axis=0), hot)
    rows = rows[:LANES] + 256.0 * rows[LANES : 2 * LANES] + 65536.0 * rows[2 * LANES :]
    inside = jnp.sum((rows < edge).astype(jnp.float32), axis=0, keepdims=True)
    whole = jnp.float32(SAMPLE_ROWS * LANES)
    place = jnp.where(before >= SAMPLE_ROWS, whole, before * LANES + inside)
    first = place[:, :SHARDS]
    count = place[:, SHARDS:] - first
    square_row, square_col = iota((SHARDS, SHARDS), 0), iota((SHARDS, SHARDS), 1)
    first_col = jnp.sum(
        jnp.where(square_row == square_col, first, 0.0), axis=1, keepdims=True
    )
    start_col = jnp.sum(
        jnp.where(square_col < square_row, count, 0.0), axis=1, keepdims=True
    )
    end_col = jnp.sum(
        jnp.where(square_col <= square_row, count, 0.0), axis=1, keepdims=True
    )
    slot = iota((1, CAP), 1).astype(jnp.float32)
    owner = jnp.sum((slot >= end_col).astype(jnp.float32), axis=0, keepdims=True)
    shard_id = iota((SHARDS, 1), 0).astype(jnp.float32)
    shift = jnp.sum(
        jnp.where(shard_id == owner, first_col - start_col, 0.0), axis=0, keepdims=True
    )
    index = slot + shift
    row = jnp.floor(index * (1.0 / LANES))
    column = index - row * LANES
    hot = (row_id == row).astype(jnp.float32).astype(jnp.bfloat16)
    bit = ((turned >> 8) & 1).astype(jnp.float32).astype(jnp.bfloat16)
    found = dot(jnp.concatenate([pieces[0], bit], axis=0), hot)
    found = found[:LANES] + 256.0 * found[LANES:]
    lane_id = iota((LANES, 1), 0).astype(jnp.float32)
    position = jnp.sum(
        jnp.where(lane_id == column, found, 0.0), axis=0, keepdims=True
    )
    used = owner < SHARDS
    code = jnp.where(used, owner * BLK + position, 0.0)
    return code.astype(jnp.int32), used.astype(jnp.float32)


def kernel(
    panel,
    signs,
    samples,
    factor,
    normalized,
    panel_v,
    signs_v,
    samples_v,
    sent,
    got,
    own_list,
    own_used,
    lists,
    codes,
    part_sent,
    part_got,
    picked,
    grams,
    local_sem,
    out_sem,
    list_sem,
    block_sem,
    part_sem,
    picked_sem,
    gram_sem,
):
    scale = 1.0 / math.sqrt(LOCAL * SHARDS)
    me = lax.axis_index("rows")
    my_col = lax.axis_index("cols")
    my_y, my_z, my_core = me >> 4, (me >> 1) & 7, me & 1
    my_lines = (my_z, my_y)
    my_sources = [my_lines[half] * 2 + my_core for half in range(2)]

    def device(half, line, core):
        if half == 0:
            return (my_y * 16 + line * 2 + core, my_col)
        return (line * 16 + my_z * 2 + core, my_col)

    def on_line(half, distance):
        return (my_lines[half] + distance) & 7

    def send(src, dst, out, arrived, target):
        pltpu.make_async_remote_copy(
            src_ref=src,
            dst_ref=dst,
            send_sem=out_sem.at[out],
            recv_sem=arrived,
            device_id=target,
            device_id_type=MESH,
        ).start()

    def wait_arrived(like, arrived):
        pltpu.make_async_copy(like, like, arrived).wait()

    def wait_left(like, out):
        pltpu.make_async_copy(like, like, out_sem.at[out]).wait()

    loads = [
        pltpu.make_async_copy(panel, panel_v, local_sem.at[2]),
        pltpu.make_async_copy(signs, signs_v, local_sem.at[1]),
        pltpu.make_async_copy(samples, samples_v, local_sem.at[0]),
    ]
    for load in loads:
        load.start()

    barrier = pltpu.get_barrier_semaphore()

    def greet(target):
        pl.semaphore_signal(barrier, inc=1, device_id=target, device_id_type=MESH)

    for distance in DISTANCES:
        for half in range(2):
            for flip in range(2):
                greet(device(half, on_line(half, distance), my_core ^ flip))
    for step in range(1, 4):
        greet((me, (my_col + step) & 3))
    greet(device(0, my_z, 1 - my_core))

    inner = hadamard_rows(iota((ORDER, ORDER), 0))
    outer = []
    for half in range(2):
        matrix = hadamard_rows(line_rows(half))
        outer.append(jnp.concatenate([matrix, matrix], axis=1))

    loads[1].wait()
    loads[0].wait()
    flip_signs = jnp.concatenate(
        [signs_v[pl.ds(j, ORDER, stride=2), :] for j in range(2)], axis=1
    )
    flip_signs = flip_signs.astype(jnp.float32) * scale

    def transform(pair):
        half = pair & 1
        values = jnp.concatenate(
            [panel_v[pl.ds(4 * j + pair, ORDER, stride=8), :] for j in range(2)],
            axis=1,
        )
        high, low = split(values * flip_signs)
        values = dot(jnp.concatenate([high, low], axis=0), inner)
        values = values[:ORDER] + values[ORDER:]
        high, low = split(values)
        values = dot(outer[half], jnp.concatenate([high, low], axis=0))
        sent[pair] = values.reshape(16, 16, ORDER)
        got[pair, my_sources[half]] = sent[pair, my_sources[half]]

    def send_block(pair, half, line, core):
        send(
            sent.at[pair, line * 2 + core],
            got.at[pair, my_sources[half]],
            1,
            block_sem.at[pair],
            device(half, line, core),
        )

    def send_blocks(first):
        for distance in DISTANCES:
            for half in range(2):
                for flip in range(2):
                    send_block(
                        first + half, half, on_line(half, distance), my_core ^ flip
                    )
        for half in range(2):
            send_block(first + half, half, my_lines[half], 1 - my_core)

    transform(0)
    transform(1)
    pl.semaphore_wait(barrier, 32)
    send_blocks(0)
    transform(2)
    transform(3)

    loads[2].wait()
    code, used = slot_list(samples_v[...], me)
    for t in range(SLOT_ROWS):
        own_list[t : t + 1, :] = code[:, t * LANES : (t + 1) * LANES]
        own_used[t : t + 1, :] = used[:, t * LANES : (t + 1) * LANES]
    own_list[SLOT_ROWS:, :] = jnp.zeros((1, LANES), jnp.int32)
    own_used[SLOT_ROWS:, :] = jnp.zeros((1, LANES), jnp.float32)
    for half in range(2):
        lists[half, my_lines[half]] = own_list[...]
        for distance in DISTANCES:
            line = on_line(half, distance)
            send(
                own_list,
                lists.at[half, my_lines[half]],
                0,
                list_sem.at[half],
                device(half, line, my_core),
            )
    send_blocks(2)

    spread = iota((8, LANES), 0) >> 1
    for half in range(2):
        wait_arrived(lists.at[half, pl.ds(0, LINE - 1)], list_sem.at[half])
        flat = lists.at[half].reshape(64, LANES)
        for t in range(SLOT_ROWS):
            rows = flat[pl.ds(t, 8, stride=8), :]
            for group in range(2):
                codes[1 - half, group, t] = jnp.take_along_axis(
                    rows, spread + 4 * group, axis=0
                )

    odd_row = iota((8, LANES), 0) & 1
    for pair in range(4):
        half = pair & 1
        other = 1 - half
        wait_arrived(got.at[pair, pl.ds(0, 15)], block_sem.at[pair])

        def add_sources(t, carry, pair=pair, half=half):
            for group in range(2):
                code = codes[half, group, t]
                lane = code & (LANES - 1)
                right = (code & LANES) != 0
                bits = (9, 10, 11, 12) if half == 0 else (9, 13, 14, 15)
                signs = [jnp.where((code & (1 << b)) != 0, -1.0, 1.0) for b in bits]

                def total(first, level):
                    if level == 0:
                        table = got[pair, first, group * 8 : group * 8 + 8, :]
                        a = jnp.take_along_axis(table[:, :LANES], lane, axis=1)
                        b = jnp.take_along_axis(table[:, LANES:], lane, axis=1)
                        return jnp.where(right, b, a)
                    upper = total(first + (1 << (level - 1)), level - 1)
                    return total(first, level - 1) + signs[level - 1] * upper

                value = total(0, 4)
                value = jnp.where(((code >> 8) & 1) == odd_row, value, 0.0)
                value = value + pltpu.roll(value, 7, 0)
                for line in range(4):
                    part_sent[pair, group * 4 + line, pl.ds(t, 1), :] = value[
                        2 * line : 2 * line + 1
                    ]
            return carry

        lax.fori_loop(0, SLOT_ROWS, add_sources, 0)

        for line in range(LINE):
            part_sent[pair, line, SLOT_ROWS:, :] = jnp.zeros((1, LANES), jnp.float32)
        for distance in DISTANCES:
            line = on_line(other, distance)
            send(
                part_sent.at[pair, line],
                part_got.at[pair, my_lines[other]],
                2,
                part_sem.at[pair],
                device(other, line, my_core),
            )
        part_got[pair, my_lines[other]] = part_sent[pair, my_lines[other]]

    wait_left(lists.at[:, pl.ds(0, LINE - 1)], 0)
    wait_left(got.at[:, pl.ds(0, 15)], 1)

    own_shard = own_list[...] >> 9
    own_mask = own_used[...]
    for pair in range(4):
        other = 1 - (pair & 1)
        shard_line = (own_shard >> 1 if other == 0 else own_shard >> 4) & 7
        wait_arrived(part_got.at[pair, pl.ds(0, LINE - 1)], part_sem.at[pair])
        total = jnp.zeros((8, LANES), jnp.float32)
        for line in range(LINE):
            value = part_got[pair, line]
            total += jnp.where(parity(shard_line & line) != 0, -value, value)
        picked[my_col, pair // 2, (pair & 1) * 8 : (pair & 1) * 8 + 8, :] = (
            total * own_mask
        )
        if pair & 1:
            for step in (2, 1, 3):
                send(
                    picked.at[my_col, pair // 2],
                    picked.at[my_col, pair // 2],
                    3,
                    picked_sem.at[pair // 2],
                    (me, (my_col + step) & 3),
                )
    wait_left(part_got.at[:, pl.ds(0, LINE - 1)], 2)
    for half in range(2):
        wait_arrived(picked.at[pl.ds(0, 3), half], picked_sem.at[half])
    flat = picked.reshape(COLS * 8, LANES)
    tiles = [flat[pl.ds(t, COLS, stride=8), :] for t in range(SLOT_ROWS)]
    panel_rows = jnp.concatenate(tiles, axis=1)

    row = iota((COLS, LANES), 0)
    lane = iota((COLS, LANES), 1)
    wide = jnp.zeros((COLS, LANES), jnp.float32)
    for j in range(COLS):
        products = tiles[0] * tiles[0][j : j + 1]
        for tile in tiles[1:]:
            products += tile * tile[j : j + 1]
        column = jnp.sum(products, axis=1, keepdims=True)
        wide = jnp.where(lane == (row & 7) * COLS + j, column, wide)
    wide = wide * (1.0 / (SAMPLE_ROWS * LANES))
    grams[me] = jnp.concatenate(
        [
            jnp.sum(wide[:8], axis=0, keepdims=True),
            jnp.sum(wide[8:], axis=0, keepdims=True),
        ],
        axis=0,
    )

    for dy, dz, core in OFFSETS:
        target = on_line(1, dy) * 16 + on_line(0, dz) * 2 + (my_core ^ core)
        send(grams.at[me], grams.at[me], 4, gram_sem.at[0], (target, my_col))
    wait_left(picked.at[pl.ds(0, 3)], 3)
    wait_arrived(grams.at[pl.ds(0, SHARDS - 1)], gram_sem.at[0])
    gram = jnp.sum(grams[...], axis=0)

    rows = jnp.concatenate(
        [jnp.broadcast_to(gram[i : i + 1], (8, LANES)) for i in range(2)], axis=0
    )
    rows = jnp.take_along_axis(rows, ((row & 7) * 16 + lane) & (LANES - 1), axis=1)
    unit = jnp.where(lane - COLS == row, 1.0, 0.0)
    both = jnp.where(lane < COLS, rows, unit)
    for j in range(COLS - 1):
        pivot_row = jnp.broadcast_to(both[j : j + 1], (COLS, LANES))
        pivot = jnp.take_along_axis(pivot_row, jnp.full_like(lane, j), axis=1)
        column = jnp.take_along_axis(both, jnp.full_like(lane, j), axis=1)
        column = jnp.where(row > j, column, 0.0)
        both = both - (column / pivot) * pivot_row
    pivots = jnp.take_along_axis(both, row, axis=1)
    both = both / jnp.sqrt(pivots)
    factor[...] = jnp.where(lane >= row, both, 0.0)[:, :COLS]

    pick_row = iota((8, COLS), 1) == iota((8, COLS), 0) + my_col * WIDTH
    own = jnp.dot(
        pick_row.astype(jnp.float32),
        both[:, COLS : 2 * COLS],
        precision=HIGHEST,
        preferred_element_type=jnp.float32,
    )
    own = jnp.dot(
        own, panel_rows, precision=HIGHEST, preferred_element_type=jnp.float32
    )
    normalized[...] = own[:WIDTH]
    wait_left(grams.at[pl.ds(0, SHARDS - 1)], 4)


def local(panel, signs, samples):
    panel = panel.reshape(WIDTH, 2 * ORDER, LANES).transpose(1, 0, 2)
    panel = panel.reshape(2 * ORDER * WIDTH, LANES)
    signs = signs.reshape(2 * ORDER, LANES)
    samples = samples.reshape(SAMPLE_ROWS, LANES)
    f32, i32, dma = jnp.float32, jnp.int32, pltpu.SemaphoreType.DMA
    factor, normalized = pl.pallas_call(
        kernel,
        out_shape=(
            jax.ShapeDtypeStruct((COLS, COLS), f32),
            jax.ShapeDtypeStruct((WIDTH, CAP), f32),
        ),
        in_specs=[pl.BlockSpec(memory_space=pltpu.HBM)] * 3,
        out_specs=[pl.BlockSpec(memory_space=pltpu.VMEM)] * 2,
        scratch_shapes=[
            pltpu.VMEM((2 * ORDER * WIDTH, LANES), f32),
            pltpu.VMEM((2 * ORDER, LANES), i32),
            pltpu.VMEM((SAMPLE_ROWS, LANES), i32),
            pltpu.VMEM((4, 16, 16, ORDER), f32),
            pltpu.VMEM((4, 16, 16, ORDER), f32),
            pltpu.VMEM((8, LANES), i32),
            pltpu.VMEM((8, LANES), f32),
            pltpu.VMEM((2, LINE, 8, LANES), i32),
            pltpu.VMEM((2, 2, SLOT_ROWS, 8, LANES), i32),
            pltpu.VMEM((4, LINE, 8, LANES), f32),
            pltpu.VMEM((4, LINE, 8, LANES), f32),
            pltpu.VMEM((4, 2, 16, LANES), f32),
            pltpu.VMEM((SHARDS, 2, LANES), f32),
            dma((3,)),
            dma((5,)),
            dma((2,)),
            dma((4,)),
            dma((4,)),
            dma((2,)),
            dma((1,)),
        ],
        compiler_params=pltpu.CompilerParams(
            collective_id=0, has_side_effects=True, vmem_limit_bytes=55100 * 1024
        ),
    )(panel, signs, samples)
    return factor, normalized


def solution(mesh):
    return jax.shard_map(
        local,
        mesh=mesh,
        in_specs=(P("cols", "rows"), P("rows"), P()),
        out_specs=(P(), P("cols", "rows")),
        check_vma=False,
    )
```

```python
import math

import jax
import jax.numpy as jnp
from jax import lax
from jax.experimental import pallas as pl
from jax.experimental.pallas import tpu as pltpu
from jax.sharding import PartitionSpec as P

LINE = 8
BLK = 512
LANES = 128
SLOT_ROWS = 7
CAP = SLOT_ROWS * LANES
WIDTH = 4
ORDER = 256
SHARDS = 128
LOCAL = ORDER * ORDER
SAMPLE_ROWS = 512
COLS = 16
MESH = pl.DeviceIdType.MESH
HIGHEST = lax.Precision.HIGHEST
DISTANCES = (4, 3, 5, 2, 6, 1, 7)
START_ORDER = sorted(
    range(SHARDS),
    key=lambda at: 1.15 * ((at >> 1) & 7) + 0.9 * min(at >> 4, 8 - (at >> 4)),
)


def iota(shape, axis):
    return lax.broadcasted_iota(jnp.int32, shape, axis)


def parity(value):
    value = value ^ (value >> 4)
    value = value ^ (value >> 2)
    value = value ^ (value >> 1)
    return value & 1


def hadamard_rows(rows):
    odd = parity(rows & iota((ORDER, ORDER), 1))
    return (1 - 2 * odd).astype(jnp.float32).astype(jnp.bfloat16)


def line_rows(half):
    place = iota((ORDER, ORDER), 0)
    line, core, other, part = place >> 5, (place >> 4) & 1, (place >> 1) & 7, place & 1
    if half == 0:
        return other * 32 + line * 4 + core * 2 + part
    return line * 32 + other * 4 + core * 2 + part


def split(values):
    high = values.astype(jnp.bfloat16)
    low = (values - high.astype(jnp.float32)).astype(jnp.bfloat16)
    return high, low


def dot(a, b):
    return jnp.dot(a, b, preferred_element_type=jnp.float32)


def slot_list(samples, device):
    turned = jnp.transpose(samples)
    pieces = [turned & 255, (turned >> 8) & 255, turned >> 16]
    pieces = [p.astype(jnp.float32).astype(jnp.bfloat16) for p in pieces]
    last = samples[:, LANES - 1 :].astype(jnp.float32)
    lane = iota((1, 2 * SHARDS), 1)
    edge = (lane & (SHARDS - 1)) * LOCAL + device * BLK + (lane >> 7) * BLK
    edge = edge.astype(jnp.float32)
    before = jnp.sum((last < edge).astype(jnp.float32), axis=0, keepdims=True)
    row_id = iota((SAMPLE_ROWS, 1), 0).astype(jnp.float32)
    hot = (row_id == before).astype(jnp.float32).astype(jnp.bfloat16)
    rows = dot(jnp.concatenate(pieces, axis=0), hot)
    rows = rows[:LANES] + 256.0 * rows[LANES : 2 * LANES] + 65536.0 * rows[2 * LANES :]
    inside = jnp.sum((rows < edge).astype(jnp.float32), axis=0, keepdims=True)
    whole = jnp.float32(SAMPLE_ROWS * LANES)
    place = jnp.where(before >= SAMPLE_ROWS, whole, before * LANES + inside)
    first = place[:, :SHARDS]
    count = place[:, SHARDS:] - first
    square_row, square_col = iota((SHARDS, SHARDS), 0), iota((SHARDS, SHARDS), 1)
    first_col = jnp.sum(
        jnp.where(square_row == square_col, first, 0.0), axis=1, keepdims=True
    )
    start_col = jnp.sum(
        jnp.where(square_col < square_row, count, 0.0), axis=1, keepdims=True
    )
    end_col = jnp.sum(
        jnp.where(square_col <= square_row, count, 0.0), axis=1, keepdims=True
    )
    slot = iota((1, CAP), 1).astype(jnp.float32)
    owner = jnp.sum((slot >= end_col).astype(jnp.float32), axis=0, keepdims=True)
    shard_id = iota((SHARDS, 1), 0).astype(jnp.float32)
    shift = jnp.sum(
        jnp.where(shard_id == owner, first_col - start_col, 0.0), axis=0, keepdims=True
    )
    index = slot + shift
    row = jnp.floor(index * (1.0 / LANES))
    column = index - row * LANES
    hot = (row_id == row).astype(jnp.float32).astype(jnp.bfloat16)
    bit = ((turned >> 8) & 1).astype(jnp.float32).astype(jnp.bfloat16)
    found = dot(jnp.concatenate([pieces[0], bit], axis=0), hot)
    found = found[:LANES] + 256.0 * found[LANES:]
    lane_id = iota((LANES, 1), 0).astype(jnp.float32)
    position = jnp.sum(
        jnp.where(lane_id == column, found, 0.0), axis=0, keepdims=True
    )
    used = owner < SHARDS
    code = jnp.where(used, owner * BLK + position, 0.0)
    return code.astype(jnp.int32), used.astype(jnp.float32)


def kernel(
    panel,
    signs,
    samples,
    factor,
    normalized,
    panel_v,
    signs_v,
    samples_v,
    sent,
    got,
    own_list,
    own_used,
    lists,
    codes,
    part_sent,
    part_got,
    picked,
    grams,
    solved,
    local_sem,
    out_sem,
    list_sem,
    block_sem,
    part_sem,
    picked_sem,
    gram_sem,
):
    scale = 1.0 / math.sqrt(LOCAL * SHARDS)
    me = lax.axis_index("rows")
    my_col = lax.axis_index("cols")
    my_y, my_z, my_core = me >> 4, (me >> 1) & 7, me & 1
    my_lines = (my_z, my_y)
    my_sources = [my_lines[half] * 2 + my_core for half in range(2)]

    def device(half, line, core):
        if half == 0:
            return (my_y * 16 + line * 2 + core, my_col)
        return (line * 16 + my_z * 2 + core, my_col)

    def on_line(half, distance):
        return (my_lines[half] + distance) & 7

    def send(src, dst, out, arrived, target):
        pltpu.make_async_remote_copy(
            src_ref=src,
            dst_ref=dst,
            send_sem=out_sem.at[out],
            recv_sem=arrived,
            device_id=target,
            device_id_type=MESH,
        ).start()

    def wait_arrived(like, arrived):
        pltpu.make_async_copy(like, like, arrived).wait()

    def wait_left(like, out):
        pltpu.make_async_copy(like, like, out_sem.at[out]).wait()

    loads = [
        pltpu.make_async_copy(panel, panel_v, local_sem.at[2]),
        pltpu.make_async_copy(signs, signs_v, local_sem.at[1]),
        pltpu.make_async_copy(samples, samples_v, local_sem.at[0]),
    ]
    for load in loads:
        load.start()

    barrier = pltpu.get_barrier_semaphore()

    def greet(target):
        pl.semaphore_signal(barrier, inc=1, device_id=target, device_id_type=MESH)

    for distance in DISTANCES:
        for half in range(2):
            for flip in range(2):
                greet(device(half, on_line(half, distance), my_core ^ flip))
    for step in range(1, 4):
        greet((me, (my_col + step) & 3))
    greet(device(0, my_z, 1 - my_core))

    inner = hadamard_rows(iota((ORDER, ORDER), 0))
    outer = []
    for half in range(2):
        matrix = hadamard_rows(line_rows(half))
        outer.append(jnp.concatenate([matrix, matrix], axis=1))

    loads[1].wait()
    loads[0].wait()
    flip_signs = jnp.concatenate(
        [signs_v[pl.ds(j, ORDER, stride=2), :] for j in range(2)], axis=1
    )
    flip_signs = flip_signs.astype(jnp.float32) * scale

    def transform(pair):
        half = pair & 1
        values = jnp.concatenate(
            [panel_v[pl.ds(4 * j + pair, ORDER, stride=8), :] for j in range(2)],
            axis=1,
        )
        high, low = split(values * flip_signs)
        values = dot(jnp.concatenate([high, low], axis=0), inner)
        values = values[:ORDER] + values[ORDER:]
        high, low = split(values)
        values = dot(outer[half], jnp.concatenate([high, low], axis=0))
        sent[pair] = values.reshape(16, 16, ORDER)
        got[pair, my_sources[half]] = sent[pair, my_sources[half]]

    def send_block(pair, half, line, core):
        send(
            sent.at[pair, line * 2 + core],
            got.at[pair, my_sources[half]],
            1,
            block_sem.at[pair],
            device(half, line, core),
        )

    def send_blocks(first):
        for distance in DISTANCES:
            for half in range(2):
                for flip in range(2):
                    send_block(
                        first + half, half, on_line(half, distance), my_core ^ flip
                    )
        for half in range(2):
            send_block(first + half, half, my_lines[half], 1 - my_core)

    transform(0)
    transform(1)
    pl.semaphore_wait(barrier, 32)
    send_blocks(0)
    transform(2)
    transform(3)

    loads[2].wait()
    code, used = slot_list(samples_v[...], me)
    for t in range(SLOT_ROWS):
        own_list[t : t + 1, :] = code[:, t * LANES : (t + 1) * LANES]
        own_used[t : t + 1, :] = used[:, t * LANES : (t + 1) * LANES]
    own_list[SLOT_ROWS:, :] = jnp.zeros((1, LANES), jnp.int32)
    own_used[SLOT_ROWS:, :] = jnp.zeros((1, LANES), jnp.float32)
    for half in range(2):
        lists[half, my_lines[half]] = own_list[...]
        for distance in DISTANCES:
            line = on_line(half, distance)
            send(
                own_list,
                lists.at[half, my_lines[half]],
                0,
                list_sem.at[half],
                device(half, line, my_core),
            )
    send_blocks(2)

    spread = iota((8, LANES), 0) >> 1
    for half in range(2):
        wait_arrived(lists.at[half, pl.ds(0, LINE - 1)], list_sem.at[half])
        flat = lists.at[half].reshape(64, LANES)
        for t in range(SLOT_ROWS):
            rows = flat[pl.ds(t, 8, stride=8), :]
            for group in range(2):
                codes[1 - half, group, t] = jnp.take_along_axis(
                    rows, spread + 4 * group, axis=0
                )

    odd_row = iota((8, LANES), 0) & 1
    for pair in range(4):
        half = pair & 1
        other = 1 - half
        wait_arrived(got.at[pair, pl.ds(0, 15)], block_sem.at[pair])

        def add_sources(t, carry, pair=pair, half=half):
            for group in range(2):
                code = codes[half, group, t]
                lane = code & (LANES - 1)
                right = (code & LANES) != 0
                bits = (9, 10, 11, 12) if half == 0 else (9, 13, 14, 15)
                signs = [jnp.where((code & (1 << b)) != 0, -1.0, 1.0) for b in bits]

                def total(first, level):
                    if level == 0:
                        table = got[pair, first, group * 8 : group * 8 + 8, :]
                        a = jnp.take_along_axis(table[:, :LANES], lane, axis=1)
                        b = jnp.take_along_axis(table[:, LANES:], lane, axis=1)
                        return jnp.where(right, b, a)
                    upper = total(first + (1 << (level - 1)), level - 1)
                    return total(first, level - 1) + signs[level - 1] * upper

                value = total(0, 4)
                value = jnp.where(((code >> 8) & 1) == odd_row, value, 0.0)
                value = value + pltpu.roll(value, 7, 0)
                for line in range(4):
                    part_sent[pair, group * 4 + line, pl.ds(t, 1), :] = value[
                        2 * line : 2 * line + 1
                    ]
            return carry

        lax.fori_loop(0, SLOT_ROWS, add_sources, 0)

        for line in range(LINE):
            part_sent[pair, line, SLOT_ROWS:, :] = jnp.zeros((1, LANES), jnp.float32)
        for distance in DISTANCES:
            line = on_line(other, distance)
            send(
                part_sent.at[pair, line],
                part_got.at[pair, my_lines[other]],
                2,
                part_sem.at[pair],
                device(other, line, my_core),
            )
        part_got[pair, my_lines[other]] = part_sent[pair, my_lines[other]]

    wait_left(lists.at[:, pl.ds(0, LINE - 1)], 0)
    wait_left(got.at[:, pl.ds(0, 15)], 1)

    own_shard = own_list[...] >> 9
    own_mask = own_used[...]
    for pair in range(4):
        other = 1 - (pair & 1)
        shard_line = (own_shard >> 1 if other == 0 else own_shard >> 4) & 7
        wait_arrived(part_got.at[pair, pl.ds(0, LINE - 1)], part_sem.at[pair])
        total = jnp.zeros((8, LANES), jnp.float32)
        for line in range(LINE):
            value = part_got[pair, line]
            total += jnp.where(parity(shard_line & line) != 0, -value, value)
        picked[my_col, pair // 2, (pair & 1) * 8 : (pair & 1) * 8 + 8, :] = (
            total * own_mask
        )
        if pair & 1:
            for step in (2, 1, 3):
                send(
                    picked.at[my_col, pair // 2],
                    picked.at[my_col, pair // 2],
                    3,
                    picked_sem.at[pair // 2],
                    (me, (my_col + step) & 3),
                )
    wait_left(part_got.at[:, pl.ds(0, LINE - 1)], 2)
    for half in range(2):
        wait_arrived(picked.at[pl.ds(0, 3), half], picked_sem.at[half])
    flat = picked.reshape(COLS * 8, LANES)
    tiles = [flat[pl.ds(t, COLS, stride=8), :] for t in range(SLOT_ROWS)]

    row = iota((COLS, LANES), 0)
    lane = iota((COLS, LANES), 1)
    wide = jnp.zeros((COLS, LANES), jnp.float32)
    for j in range(COLS):
        products = tiles[0] * tiles[0][j : j + 1]
        for tile in tiles[1:]:
            products += tile * tile[j : j + 1]
        column = jnp.sum(products, axis=1, keepdims=True)
        wide = jnp.where(lane == (row & 7) * COLS + j, column, wide)
    wide = wide * (1.0 / (SAMPLE_ROWS * LANES))
    grams[me] = jnp.concatenate(
        [
            jnp.sum(wide[:8], axis=0, keepdims=True),
            jnp.sum(wide[8:], axis=0, keepdims=True),
        ],
        axis=0,
    )

    for target in START_ORDER:

        @pl.when(me != target)
        def _(target=target):
            send(grams.at[me], grams.at[me], 4, gram_sem.at[0], (target, my_col))

    wait_left(picked.at[pl.ds(0, 3)], 3)
    wait_arrived(grams.at[pl.ds(0, SHARDS - 1)], gram_sem.at[0])
    gram = jnp.sum(grams[...], axis=0)

    rows = jnp.concatenate(
        [jnp.broadcast_to(gram[i : i + 1], (8, LANES)) for i in range(2)], axis=0
    )
    rows = jnp.take_along_axis(rows, ((row & 7) * 16 + lane) & (LANES - 1), axis=1)
    columns = [
        jnp.take_along_axis(rows, jnp.full_like(lane, j), axis=1) for j in range(COLS)
    ]
    values = [flat[8 * j : 8 * j + 8, :] for j in range(COLS)]
    upper = jnp.zeros((COLS, LANES), jnp.float32)
    roots = jnp.zeros((COLS, LANES), jnp.float32)
    for j in range(COLS):
        pivot = columns[j][j : j + 1]
        share = jnp.where(row > j, columns[j] * (1.0 / pivot), 0.0)
        for k in range(j + 1, COLS):
            columns[k] -= share * columns[k][j : j + 1]
            values[k] -= share[k : k + 1] * values[j]
        root = 1.0 / jnp.sqrt(pivot)
        solved[j] = values[j] * root
        roots = jnp.where(row == j, root, roots)
        upper = jnp.where((lane == j) & (row <= j), columns[j], upper)
    factor[...] = (upper * roots)[:, :COLS]
    for column in range(WIDTH):
        own = solved[my_col * WIDTH + column]
        for t in range(SLOT_ROWS):
            normalized[column : column + 1, t * LANES : (t + 1) * LANES] = own[t : t + 1]
    wait_left(grams.at[pl.ds(0, SHARDS - 1)], 4)


def local(panel, signs, samples):
    panel = panel.reshape(WIDTH, 2 * ORDER, LANES).transpose(1, 0, 2)
    panel = panel.reshape(2 * ORDER * WIDTH, LANES)
    signs = signs.reshape(2 * ORDER, LANES)
    samples = samples.reshape(SAMPLE_ROWS, LANES)
    f32, i32, dma = jnp.float32, jnp.int32, pltpu.SemaphoreType.DMA
    factor, normalized = pl.pallas_call(
        kernel,
        out_shape=(
            jax.ShapeDtypeStruct((COLS, COLS), f32),
            jax.ShapeDtypeStruct((WIDTH, CAP), f32),
        ),
        in_specs=[pl.BlockSpec(memory_space=pltpu.HBM)] * 3,
        out_specs=[pl.BlockSpec(memory_space=pltpu.VMEM)] * 2,
        scratch_shapes=[
            pltpu.VMEM((2 * ORDER * WIDTH, LANES), f32),
            pltpu.VMEM((2 * ORDER, LANES), i32),
            pltpu.VMEM((SAMPLE_ROWS, LANES), i32),
            pltpu.VMEM((4, 16, 16, ORDER), f32),
            pltpu.VMEM((4, 16, 16, ORDER), f32),
            pltpu.VMEM((8, LANES), i32),
            pltpu.VMEM((8, LANES), f32),
            pltpu.VMEM((2, LINE, 8, LANES), i32),
            pltpu.VMEM((2, 2, SLOT_ROWS, 8, LANES), i32),
            pltpu.VMEM((4, LINE, 8, LANES), f32),
            pltpu.VMEM((4, LINE, 8, LANES), f32),
            pltpu.VMEM((4, 2, 16, LANES), f32),
            pltpu.VMEM((SHARDS, 2, LANES), f32),
            pltpu.VMEM((COLS, 8, LANES), f32),
            dma((3,)),
            dma((5,)),
            dma((2,)),
            dma((4,)),
            dma((4,)),
            dma((2,)),
            dma((1,)),
        ],
        compiler_params=pltpu.CompilerParams(
            collective_id=0, has_side_effects=True, vmem_limit_bytes=55100 * 1024
        ),
    )(panel, signs, samples)
    return factor, normalized


def solution(mesh):
    return jax.shard_map(
        local,
        mesh=mesh,
        in_specs=(P("cols", "rows"), P("rows"), P()),
        out_specs=(P(), P("cols", "rows")),
        check_vma=False,
    )
```

```python
import math

import jax
import jax.numpy as jnp
from jax import lax
from jax.experimental import pallas as pl
from jax.experimental.pallas import tpu as pltpu
from jax.sharding import PartitionSpec as P

LINE = 8
BLK = 512
LANES = 128
SLOT_ROWS = 7
CAP = SLOT_ROWS * LANES
WIDTH = 4
ORDER = 256
SHARDS = 128
LOCAL = ORDER * ORDER
SAMPLE_ROWS = 512
COLS = 16
MESH = pl.DeviceIdType.MESH
HIGHEST = lax.Precision.HIGHEST
DISTANCES = (4, 3, 5, 2, 6, 1, 7)
START_ORDER = sorted(
    range(SHARDS),
    key=lambda at: 1.15 * ((at >> 1) & 7) + 0.9 * min(at >> 4, 8 - (at >> 4)),
)


def iota(shape, axis):
    return lax.broadcasted_iota(jnp.int32, shape, axis)


def parity(value):
    value = value ^ (value >> 4)
    value = value ^ (value >> 2)
    value = value ^ (value >> 1)
    return value & 1


def hadamard_rows(rows):
    odd = parity(rows & iota((ORDER, ORDER), 1))
    return (1 - 2 * odd).astype(jnp.float32).astype(jnp.bfloat16)


def line_rows(half):
    place = iota((ORDER, ORDER), 0)
    line, core, other, part = place >> 5, (place >> 4) & 1, (place >> 1) & 7, place & 1
    if half == 0:
        return other * 32 + line * 4 + core * 2 + part
    return line * 32 + other * 4 + core * 2 + part


def split(values):
    high = values.astype(jnp.bfloat16)
    low = (values - high.astype(jnp.float32)).astype(jnp.bfloat16)
    return high, low


def dot(a, b):
    return jnp.dot(a, b, preferred_element_type=jnp.float32)


def slot_list(samples, device):
    turned = jnp.transpose(samples)
    pieces = [turned & 255, (turned >> 8) & 255, turned >> 16]
    pieces = [p.astype(jnp.float32).astype(jnp.bfloat16) for p in pieces]
    last = samples[:, LANES - 1 :].astype(jnp.float32)
    lane = iota((1, 2 * SHARDS), 1)
    edge = (lane & (SHARDS - 1)) * LOCAL + device * BLK + (lane >> 7) * BLK
    edge = edge.astype(jnp.float32)
    before = jnp.sum((last < edge).astype(jnp.float32), axis=0, keepdims=True)
    row_id = iota((SAMPLE_ROWS, 1), 0).astype(jnp.float32)
    hot = (row_id == before).astype(jnp.float32).astype(jnp.bfloat16)
    rows = dot(jnp.concatenate(pieces, axis=0), hot)
    rows = rows[:LANES] + 256.0 * rows[LANES : 2 * LANES] + 65536.0 * rows[2 * LANES :]
    inside = jnp.sum((rows < edge).astype(jnp.float32), axis=0, keepdims=True)
    whole = jnp.float32(SAMPLE_ROWS * LANES)
    place = jnp.where(before >= SAMPLE_ROWS, whole, before * LANES + inside)
    first = place[:, :SHARDS]
    count = place[:, SHARDS:] - first
    square_row, square_col = iota((SHARDS, SHARDS), 0), iota((SHARDS, SHARDS), 1)
    first_col = jnp.sum(
        jnp.where(square_row == square_col, first, 0.0), axis=1, keepdims=True
    )
    start_col = jnp.sum(
        jnp.where(square_col < square_row, count, 0.0), axis=1, keepdims=True
    )
    end_col = jnp.sum(
        jnp.where(square_col <= square_row, count, 0.0), axis=1, keepdims=True
    )
    slot = iota((1, CAP), 1).astype(jnp.float32)
    owner = jnp.sum((slot >= end_col).astype(jnp.float32), axis=0, keepdims=True)
    shard_id = iota((SHARDS, 1), 0).astype(jnp.float32)
    shift = jnp.sum(
        jnp.where(shard_id == owner, first_col - start_col, 0.0), axis=0, keepdims=True
    )
    index = slot + shift
    row = jnp.floor(index * (1.0 / LANES))
    column = index - row * LANES
    hot = (row_id == row).astype(jnp.float32).astype(jnp.bfloat16)
    bit = ((turned >> 8) & 1).astype(jnp.float32).astype(jnp.bfloat16)
    found = dot(jnp.concatenate([pieces[0], bit], axis=0), hot)
    found = found[:LANES] + 256.0 * found[LANES:]
    lane_id = iota((LANES, 1), 0).astype(jnp.float32)
    position = jnp.sum(
        jnp.where(lane_id == column, found, 0.0), axis=0, keepdims=True
    )
    used = owner < SHARDS
    code = jnp.where(used, owner * BLK + position, 0.0)
    return code.astype(jnp.int32), used.astype(jnp.float32)


def kernel(
    panel,
    signs,
    samples,
    factor,
    normalized,
    panel_v,
    signs_v,
    samples_v,
    sent,
    got,
    own_list,
    own_used,
    lists,
    codes,
    part_sent,
    part_got,
    picked,
    grams,
    solved,
    local_sem,
    out_sem,
    list_sem,
    block_sem,
    part_sem,
    picked_sem,
    gram_sem,
):
    scale = 1.0 / math.sqrt(LOCAL * SHARDS)
    me = lax.axis_index("rows")
    my_col = lax.axis_index("cols")
    my_y, my_z, my_core = me >> 4, (me >> 1) & 7, me & 1
    my_lines = (my_z, my_y)
    my_sources = [my_lines[half] * 2 + my_core for half in range(2)]

    def device(half, line, core):
        if half == 0:
            return (my_y * 16 + line * 2 + core, my_col)
        return (line * 16 + my_z * 2 + core, my_col)

    def on_line(half, distance):
        return (my_lines[half] + distance) & 7

    def send(src, dst, out, arrived, target):
        pltpu.make_async_remote_copy(
            src_ref=src,
            dst_ref=dst,
            send_sem=out_sem.at[out],
            recv_sem=arrived,
            device_id=target,
            device_id_type=MESH,
        ).start()

    def wait_arrived(like, arrived):
        pltpu.make_async_copy(like, like, arrived).wait()

    def wait_left(like, out):
        pltpu.make_async_copy(like, like, out_sem.at[out]).wait()

    loads = [
        pltpu.make_async_copy(panel, panel_v, local_sem.at[2]),
        pltpu.make_async_copy(signs, signs_v, local_sem.at[1]),
        pltpu.make_async_copy(samples, samples_v, local_sem.at[0]),
    ]
    for load in loads:
        load.start()

    barrier = pltpu.get_barrier_semaphore()

    def greet(target):
        pl.semaphore_signal(barrier, inc=1, device_id=target, device_id_type=MESH)

    for distance in DISTANCES:
        for half in range(2):
            for flip in range(2):
                greet(device(half, on_line(half, distance), my_core ^ flip))
    for step in range(1, 4):
        greet((me, (my_col + step) & 3))
    greet(device(0, my_z, 1 - my_core))

    inner = hadamard_rows(iota((ORDER, ORDER), 0))
    outer = []
    for half in range(2):
        matrix = hadamard_rows(line_rows(half))
        outer.append(jnp.concatenate([matrix, matrix], axis=1))

    loads[1].wait()
    loads[0].wait()
    flip_signs = jnp.concatenate(
        [signs_v[pl.ds(j, ORDER, stride=2), :] for j in range(2)], axis=1
    )
    flip_signs = flip_signs.astype(jnp.float32) * scale

    def transform(pair):
        half = pair & 1
        values = jnp.concatenate(
            [panel_v[pl.ds(4 * j + pair, ORDER, stride=8), :] for j in range(2)],
            axis=1,
        )
        high, low = split(values * flip_signs)
        values = dot(jnp.concatenate([high, low], axis=0), inner)
        values = values[:ORDER] + values[ORDER:]
        high, low = split(values)
        values = dot(outer[half], jnp.concatenate([high, low], axis=0))
        sent[pair] = values.reshape(16, 16, ORDER)
        got[pair, my_sources[half]] = sent[pair, my_sources[half]]

    def send_block(pair, half, line, core):
        send(
            sent.at[pair, line * 2 + core],
            got.at[pair, my_sources[half]],
            1,
            block_sem.at[pair],
            device(half, line, core),
        )

    def send_blocks(first):
        for distance in DISTANCES:
            for half in range(2):
                for flip in range(2):
                    send_block(
                        first + half, half, on_line(half, distance), my_core ^ flip
                    )
        for half in range(2):
            send_block(first + half, half, my_lines[half], 1 - my_core)

    transform(0)
    transform(1)
    pl.semaphore_wait(barrier, 32)
    send_blocks(0)
    transform(2)
    transform(3)

    loads[2].wait()
    code, used = slot_list(samples_v[...], me)
    for t in range(SLOT_ROWS):
        own_list[t : t + 1, :] = code[:, t * LANES : (t + 1) * LANES]
        own_used[t : t + 1, :] = used[:, t * LANES : (t + 1) * LANES]
    own_list[SLOT_ROWS:, :] = jnp.zeros((1, LANES), jnp.int32)
    own_used[SLOT_ROWS:, :] = jnp.zeros((1, LANES), jnp.float32)
    for half in range(2):
        lists[half, my_lines[half]] = own_list[...]
        for distance in DISTANCES:
            line = on_line(half, distance)
            send(
                own_list,
                lists.at[half, my_lines[half]],
                0,
                list_sem.at[half],
                device(half, line, my_core),
            )
    send_blocks(2)

    spread = iota((8, LANES), 0) >> 1
    for half in range(2):
        wait_arrived(lists.at[half, pl.ds(0, LINE - 1)], list_sem.at[half])
        flat = lists.at[half].reshape(64, LANES)
        for t in range(SLOT_ROWS):
            rows = flat[pl.ds(t, 8, stride=8), :]
            for group in range(2):
                codes[1 - half, group, t] = jnp.take_along_axis(
                    rows, spread + 4 * group, axis=0
                )

    odd_row = iota((8, LANES), 0) & 1
    for pair in range(4):
        half = pair & 1
        other = 1 - half
        wait_arrived(got.at[pair, pl.ds(0, 15)], block_sem.at[pair])

        def add_sources(t, carry, pair=pair, half=half):
            for group in range(2):
                code = codes[half, group, t]
                lane = code & (LANES - 1)
                right = (code & LANES) != 0
                bits = (9, 10, 11, 12) if half == 0 else (9, 13, 14, 15)
                signs = [jnp.where((code & (1 << b)) != 0, -1.0, 1.0) for b in bits]

                def total(first, level):
                    if level == 0:
                        table = got[pair, first, group * 8 : group * 8 + 8, :]
                        a = jnp.take_along_axis(table[:, :LANES], lane, axis=1)
                        b = jnp.take_along_axis(table[:, LANES:], lane, axis=1)
                        return jnp.where(right, b, a)
                    upper = total(first + (1 << (level - 1)), level - 1)
                    return total(first, level - 1) + signs[level - 1] * upper

                value = total(0, 4)
                value = jnp.where(((code >> 8) & 1) == odd_row, value, 0.0)
                value = value + pltpu.roll(value, 7, 0)
                for line in range(4):
                    part_sent[pair, group * 4 + line, pl.ds(t, 1), :] = value[
                        2 * line : 2 * line + 1
                    ]
            return carry

        lax.fori_loop(0, SLOT_ROWS, add_sources, 0, unroll=True)

        for line in range(LINE):
            part_sent[pair, line, SLOT_ROWS:, :] = jnp.zeros((1, LANES), jnp.float32)
        for distance in DISTANCES:
            line = on_line(other, distance)
            send(
                part_sent.at[pair, line],
                part_got.at[pair, my_lines[other]],
                2,
                part_sem.at[pair],
                device(other, line, my_core),
            )
        part_got[pair, my_lines[other]] = part_sent[pair, my_lines[other]]

    wait_left(lists.at[:, pl.ds(0, LINE - 1)], 0)
    wait_left(got.at[:, pl.ds(0, 15)], 1)

    own_shard = own_list[...] >> 9
    own_mask = own_used[...]
    for pair in range(4):
        other = 1 - (pair & 1)
        shard_line = (own_shard >> 1 if other == 0 else own_shard >> 4) & 7
        wait_arrived(part_got.at[pair, pl.ds(0, LINE - 1)], part_sem.at[pair])
        total = jnp.zeros((8, LANES), jnp.float32)
        for line in range(LINE):
            value = part_got[pair, line]
            total += jnp.where(parity(shard_line & line) != 0, -value, value)
        picked[my_col, pair // 2, (pair & 1) * 8 : (pair & 1) * 8 + 8, :] = (
            total * own_mask
        )
        if pair & 1:
            for step in (2, 1, 3):
                send(
                    picked.at[my_col, pair // 2],
                    picked.at[my_col, pair // 2],
                    3,
                    picked_sem.at[pair // 2],
                    (me, (my_col + step) & 3),
                )
    wait_left(part_got.at[:, pl.ds(0, LINE - 1)], 2)
    for half in range(2):
        wait_arrived(picked.at[pl.ds(0, 3), half], picked_sem.at[half])
    flat = picked.reshape(COLS * 8, LANES)
    tiles = [flat[pl.ds(t, COLS, stride=8), :] for t in range(SLOT_ROWS)]

    row = iota((COLS, LANES), 0)
    lane = iota((COLS, LANES), 1)
    wide = jnp.zeros((COLS, LANES), jnp.float32)
    for j in range(COLS):
        products = tiles[0] * tiles[0][j : j + 1]
        for tile in tiles[1:]:
            products += tile * tile[j : j + 1]
        column = jnp.sum(products, axis=1, keepdims=True)
        wide = jnp.where(lane == (row & 7) * COLS + j, column, wide)
    wide = wide * (1.0 / (SAMPLE_ROWS * LANES))
    grams[me] = jnp.concatenate(
        [
            jnp.sum(wide[:8], axis=0, keepdims=True),
            jnp.sum(wide[8:], axis=0, keepdims=True),
        ],
        axis=0,
    )

    for target in START_ORDER:

        @pl.when(me != target)
        def _(target=target):
            send(grams.at[me], grams.at[me], 4, gram_sem.at[0], (target, my_col))

    wait_left(picked.at[pl.ds(0, 3)], 3)
    wait_arrived(grams.at[pl.ds(0, SHARDS - 1)], gram_sem.at[0])
    gram = jnp.sum(grams[...], axis=0)

    rows = jnp.concatenate(
        [jnp.broadcast_to(gram[i : i + 1], (8, LANES)) for i in range(2)], axis=0
    )
    rows = jnp.take_along_axis(rows, ((row & 7) * 16 + lane) & (LANES - 1), axis=1)
    columns = [
        jnp.take_along_axis(rows, jnp.full_like(lane, j), axis=1) for j in range(COLS)
    ]
    values = [flat[8 * j : 8 * j + 8, :] for j in range(COLS)]
    upper = jnp.zeros((COLS, LANES), jnp.float32)
    roots = jnp.zeros((COLS, LANES), jnp.float32)
    for j in range(COLS):
        pivot = columns[j][j : j + 1]
        share = jnp.where(row > j, columns[j] * (1.0 / pivot), 0.0)
        for k in range(j + 1, COLS):
            columns[k] -= share * columns[k][j : j + 1]
            values[k] -= share[k : k + 1] * values[j]
        root = 1.0 / jnp.sqrt(pivot)
        solved[j] = values[j] * root
        roots = jnp.where(row == j, root, roots)
        upper = jnp.where((lane == j) & (row <= j), columns[j], upper)
    factor[...] = (upper * roots)[:, :COLS]
    for column in range(WIDTH):
        own = solved[my_col * WIDTH + column]
        for t in range(SLOT_ROWS):
            normalized[column : column + 1, t * LANES : (t + 1) * LANES] = own[t : t + 1]
    wait_left(grams.at[pl.ds(0, SHARDS - 1)], 4)


def local(panel, signs, samples):
    panel = panel.reshape(WIDTH, 2 * ORDER, LANES).transpose(1, 0, 2)
    panel = panel.reshape(2 * ORDER * WIDTH, LANES)
    signs = signs.reshape(2 * ORDER, LANES)
    samples = samples.reshape(SAMPLE_ROWS, LANES)
    f32, i32, dma = jnp.float32, jnp.int32, pltpu.SemaphoreType.DMA
    factor, normalized = pl.pallas_call(
        kernel,
        out_shape=(
            jax.ShapeDtypeStruct((COLS, COLS), f32),
            jax.ShapeDtypeStruct((WIDTH, CAP), f32),
        ),
        in_specs=[pl.BlockSpec(memory_space=pltpu.HBM)] * 3,
        out_specs=[pl.BlockSpec(memory_space=pltpu.VMEM)] * 2,
        scratch_shapes=[
            pltpu.VMEM((2 * ORDER * WIDTH, LANES), f32),
            pltpu.VMEM((2 * ORDER, LANES), i32),
            pltpu.VMEM((SAMPLE_ROWS, LANES), i32),
            pltpu.VMEM((4, 16, 16, ORDER), f32),
            pltpu.VMEM((4, 16, 16, ORDER), f32),
            pltpu.VMEM((8, LANES), i32),
            pltpu.VMEM((8, LANES), f32),
            pltpu.VMEM((2, LINE, 8, LANES), i32),
            pltpu.VMEM((2, 2, SLOT_ROWS, 8, LANES), i32),
            pltpu.VMEM((4, LINE, 8, LANES), f32),
            pltpu.VMEM((4, LINE, 8, LANES), f32),
            pltpu.VMEM((4, 2, 16, LANES), f32),
            pltpu.VMEM((SHARDS, 2, LANES), f32),
            pltpu.VMEM((COLS, 8, LANES), f32),
            dma((3,)),
            dma((5,)),
            dma((2,)),
            dma((4,)),
            dma((4,)),
            dma((2,)),
            dma((1,)),
        ],
        compiler_params=pltpu.CompilerParams(
            collective_id=0, has_side_effects=True, vmem_limit_bytes=55100 * 1024
        ),
    )(panel, signs, samples)
    return factor, normalized


def solution(mesh):
    return jax.shard_map(
        local,
        mesh=mesh,
        in_specs=(P("cols", "rows"), P("rows"), P()),
        out_specs=(P(), P("cols", "rows")),
        check_vma=False,
    )
```

```python
import math

import jax
import jax.numpy as jnp
from jax import lax
from jax.experimental import pallas as pl
from jax.experimental.pallas import tpu as pltpu
from jax.sharding import PartitionSpec as P

LINE = 8
BLK = 512
LANES = 128
SLOT_ROWS = 7
CAP = SLOT_ROWS * LANES
WIDTH = 4
ORDER = 256
SHARDS = 128
LOCAL = ORDER * ORDER
SAMPLE_ROWS = 512
COLS = 16
MESH = pl.DeviceIdType.MESH
HIGHEST = lax.Precision.HIGHEST
DISTANCES = (4, 3, 5, 2, 6, 1, 7)
START_ORDER = sorted(
    range(SHARDS),
    key=lambda at: 1.15 * ((at >> 1) & 7) + 0.9 * min(at >> 4, 8 - (at >> 4)),
)


def iota(shape, axis):
    return lax.broadcasted_iota(jnp.int32, shape, axis)


def parity(value):
    value = value ^ (value >> 4)
    value = value ^ (value >> 2)
    value = value ^ (value >> 1)
    return value & 1


def hadamard_rows(rows):
    odd = parity(rows & iota((ORDER, ORDER), 1))
    return (1 - 2 * odd).astype(jnp.float32).astype(jnp.bfloat16)


def line_rows(half):
    place = iota((ORDER, ORDER), 0)
    line, core, other, part = place >> 5, (place >> 4) & 1, (place >> 1) & 7, place & 1
    if half == 0:
        return other * 32 + line * 4 + core * 2 + part
    return line * 32 + other * 4 + core * 2 + part


def split(values):
    high = values.astype(jnp.bfloat16)
    low = (values - high.astype(jnp.float32)).astype(jnp.bfloat16)
    return high, low


def dot(a, b):
    return jnp.dot(a, b, preferred_element_type=jnp.float32)


def slot_list(samples, device):
    turned = jnp.transpose(samples)
    pieces = [turned & 255, (turned >> 8) & 255, turned >> 16]
    pieces = [p.astype(jnp.float32).astype(jnp.bfloat16) for p in pieces]
    last = samples[:, LANES - 1 :].astype(jnp.float32)
    lane = iota((1, 2 * SHARDS), 1)
    edge = (lane & (SHARDS - 1)) * LOCAL + device * BLK + (lane >> 7) * BLK
    edge = edge.astype(jnp.float32)
    before = jnp.sum((last < edge).astype(jnp.float32), axis=0, keepdims=True)
    row_id = iota((SAMPLE_ROWS, 1), 0).astype(jnp.float32)
    hot = (row_id == before).astype(jnp.float32).astype(jnp.bfloat16)
    rows = dot(jnp.concatenate(pieces, axis=0), hot)
    rows = rows[:LANES] + 256.0 * rows[LANES : 2 * LANES] + 65536.0 * rows[2 * LANES :]
    inside = jnp.sum((rows < edge).astype(jnp.float32), axis=0, keepdims=True)
    whole = jnp.float32(SAMPLE_ROWS * LANES)
    place = jnp.where(before >= SAMPLE_ROWS, whole, before * LANES + inside)
    first = place[:, :SHARDS]
    count = place[:, SHARDS:] - first
    square_row, square_col = iota((SHARDS, SHARDS), 0), iota((SHARDS, SHARDS), 1)
    first_col = jnp.sum(
        jnp.where(square_row == square_col, first, 0.0), axis=1, keepdims=True
    )
    start_col = jnp.sum(
        jnp.where(square_col < square_row, count, 0.0), axis=1, keepdims=True
    )
    end_col = jnp.sum(
        jnp.where(square_col <= square_row, count, 0.0), axis=1, keepdims=True
    )
    slot = iota((1, CAP), 1).astype(jnp.float32)
    owner = jnp.sum((slot >= end_col).astype(jnp.float32), axis=0, keepdims=True)
    shard_id = iota((SHARDS, 1), 0).astype(jnp.float32)
    shift = jnp.sum(
        jnp.where(shard_id == owner, first_col - start_col, 0.0), axis=0, keepdims=True
    )
    index = slot + shift
    row = jnp.floor(index * (1.0 / LANES))
    column = index - row * LANES
    hot = (row_id == row).astype(jnp.float32).astype(jnp.bfloat16)
    bit = ((turned >> 8) & 1).astype(jnp.float32).astype(jnp.bfloat16)
    found = dot(jnp.concatenate([pieces[0], bit], axis=0), hot)
    found = found[:LANES] + 256.0 * found[LANES:]
    lane_id = iota((LANES, 1), 0).astype(jnp.float32)
    position = jnp.sum(
        jnp.where(lane_id == column, found, 0.0), axis=0, keepdims=True
    )
    used = owner < SHARDS
    code = jnp.where(used, owner * BLK + position, 0.0)
    return code.astype(jnp.int32), used.astype(jnp.float32)


def kernel(
    panel,
    signs,
    samples,
    factor,
    normalized,
    panel_v,
    signs_v,
    samples_v,
    sent,
    got,
    own_list,
    own_used,
    lists,
    codes,
    part_sent,
    part_got,
    picked,
    grams,
    solved,
    local_sem,
    out_sem,
    list_sem,
    block_sem,
    part_sem,
    picked_sem,
    gram_sem,
):
    scale = 1.0 / math.sqrt(LOCAL * SHARDS)
    me = lax.axis_index("rows")
    my_col = lax.axis_index("cols")
    my_y, my_z, my_core = me >> 4, (me >> 1) & 7, me & 1
    my_lines = (my_z, my_y)
    my_sources = [my_lines[half] * 2 + my_core for half in range(2)]

    def device(half, line, core):
        if half == 0:
            return (my_y * 16 + line * 2 + core, my_col)
        return (line * 16 + my_z * 2 + core, my_col)

    def on_line(half, distance):
        return (my_lines[half] + distance) & 7

    def send(src, dst, out, arrived, target):
        pltpu.make_async_remote_copy(
            src_ref=src,
            dst_ref=dst,
            send_sem=out_sem.at[out],
            recv_sem=arrived,
            device_id=target,
            device_id_type=MESH,
        ).start()

    def wait_arrived(like, arrived):
        pltpu.make_async_copy(like, like, arrived).wait()

    def wait_left(like, out):
        pltpu.make_async_copy(like, like, out_sem.at[out]).wait()

    barrier = pltpu.get_barrier_semaphore()

    def greet(target):
        pl.semaphore_signal(barrier, inc=1, device_id=target, device_id_type=MESH)

    for distance in DISTANCES:
        for half in range(2):
            for flip in range(2):
                greet(device(half, on_line(half, distance), my_core ^ flip))
    for step in range(1, 4):
        greet((me, (my_col + step) & 3))
    greet(device(0, my_z, 1 - my_core))

    loads = [
        pltpu.make_async_copy(panel, panel_v, local_sem.at[2]),
        pltpu.make_async_copy(signs, signs_v, local_sem.at[1]),
        pltpu.make_async_copy(samples, samples_v, local_sem.at[0]),
    ]
    for load in loads:
        load.start()

    inner = hadamard_rows(iota((ORDER, ORDER), 0))
    outer = []
    for half in range(2):
        matrix = hadamard_rows(line_rows(half))
        outer.append(jnp.concatenate([matrix, matrix], axis=1))

    loads[1].wait()
    loads[0].wait()
    flip_signs = jnp.concatenate(
        [signs_v[pl.ds(j, ORDER, stride=2), :] for j in range(2)], axis=1
    )
    flip_signs = flip_signs.astype(jnp.float32) * scale

    def transform(pair):
        half = pair & 1
        values = jnp.concatenate(
            [panel_v[pl.ds(4 * j + pair, ORDER, stride=8), :] for j in range(2)],
            axis=1,
        )
        high, low = split(values * flip_signs)
        values = dot(jnp.concatenate([high, low], axis=0), inner)
        values = values[:ORDER] + values[ORDER:]
        high, low = split(values)
        values = dot(outer[half], jnp.concatenate([high, low], axis=0))
        sent[pair] = values.reshape(16, 16, ORDER)
        got[pair, my_sources[half]] = sent[pair, my_sources[half]]

    def send_block(pair, half, line, core, rows, arrived):
        send(
            sent.at[pair, line * 2 + core, rows],
            got.at[pair, my_sources[half], rows],
            1,
            block_sem.at[arrived],
            device(half, line, core),
        )

    def send_blocks(first, rows, arrived):
        for distance in DISTANCES:
            for half in range(2):
                for flip in range(2):
                    line = on_line(half, distance)
                    send_block(
                        first + half, half, line, my_core ^ flip, rows, arrived + half
                    )
        for half in range(2):
            send_block(
                first + half, half, my_lines[half], 1 - my_core, rows, arrived + half
            )

    transform(0)
    transform(1)
    pl.semaphore_wait(barrier, 32)
    send_blocks(0, pl.ds(0, 16), 0)
    transform(2)
    transform(3)

    loads[2].wait()
    code, used = slot_list(samples_v[...], me)
    for t in range(SLOT_ROWS):
        own_list[t : t + 1, :] = code[:, t * LANES : (t + 1) * LANES]
        own_used[t : t + 1, :] = used[:, t * LANES : (t + 1) * LANES]
    own_list[SLOT_ROWS:, :] = jnp.zeros((1, LANES), jnp.int32)
    own_used[SLOT_ROWS:, :] = jnp.zeros((1, LANES), jnp.float32)
    for half in range(2):
        lists[half, my_lines[half]] = own_list[...]
        for distance in DISTANCES:
            line = on_line(half, distance)
            send(
                own_list,
                lists.at[half, my_lines[half]],
                0,
                list_sem.at[half],
                device(half, line, my_core),
            )
    for group in range(2):
        send_blocks(2, pl.ds(8 * group, 8), 2 + 2 * group)

    spread = iota((8, LANES), 0) >> 1
    for half in range(2):
        wait_arrived(lists.at[half, pl.ds(0, LINE - 1)], list_sem.at[half])
        flat = lists.at[half].reshape(64, LANES)
        for t in range(SLOT_ROWS):
            rows = flat[pl.ds(t, 8, stride=8), :]
            for group in range(2):
                codes[1 - half, group, t] = jnp.take_along_axis(
                    rows, spread + 4 * group, axis=0
                )

    odd_row = iota((8, LANES), 0) & 1
    def sample(pair, groups):
        half = pair & 1

        def add_sources(t, carry):
            for group in groups:
                code = codes[half, group, t]
                lane = code & (LANES - 1)
                right = (code & LANES) != 0
                bits = (9, 10, 11, 12) if half == 0 else (9, 13, 14, 15)
                signs = [jnp.where((code & (1 << b)) != 0, -1.0, 1.0) for b in bits]

                def total(first, level):
                    if level == 0:
                        table = got[pair, first, group * 8 : group * 8 + 8, :]
                        a = jnp.take_along_axis(table[:, :LANES], lane, axis=1)
                        b = jnp.take_along_axis(table[:, LANES:], lane, axis=1)
                        return jnp.where(right, b, a)
                    upper = total(first + (1 << (level - 1)), level - 1)
                    return total(first, level - 1) + signs[level - 1] * upper

                value = total(0, 4)
                value = jnp.where(((code >> 8) & 1) == odd_row, value, 0.0)
                value = value + pltpu.roll(value, 7, 0)
                for line in range(4):
                    part_sent[pair, group * 4 + line, pl.ds(t, 1), :] = value[
                        2 * line : 2 * line + 1
                    ]
            return carry

        lax.fori_loop(0, SLOT_ROWS, add_sources, 0, unroll=True)
        for group in groups:
            for line in range(4 * group, 4 * group + 4):
                part_sent[pair, line, SLOT_ROWS:, :] = jnp.zeros(
                    (1, LANES), jnp.float32
                )

    def send_sums(pair, line):
        other = 1 - (pair & 1)
        send(
            part_sent.at[pair, line],
            part_got.at[pair, my_lines[other]],
            2,
            part_sem.at[pair],
            device(other, line, my_core),
        )

    for pair in range(2):
        other = 1 - pair
        wait_arrived(got.at[pair, pl.ds(0, 15)], block_sem.at[pair])
        sample(pair, (0, 1))
        for distance in DISTANCES:
            send_sums(pair, on_line(other, distance))
        part_got[pair, my_lines[other]] = part_sent[pair, my_lines[other]]
    for group in range(2):
        for pair in range(2, 4):
            other = 1 - (pair & 1)
            wait_arrived(
                got.at[pair, pl.ds(0, 15), pl.ds(0, 8)], block_sem.at[pair + 2 * group]
            )
            sample(pair, (group,))
            for line in range(4 * group, 4 * group + 4):

                @pl.when(line != my_lines[other])
                def _(pair=pair, line=line):
                    send_sums(pair, line)

    for pair in range(2, 4):
        other = 1 - (pair & 1)
        part_got[pair, my_lines[other]] = part_sent[pair, my_lines[other]]

    wait_left(lists.at[:, pl.ds(0, LINE - 1)], 0)
    wait_left(got.at[:, pl.ds(0, 15)], 1)

    own_shard = own_list[...] >> 9
    own_mask = own_used[...]
    for pair in range(4):
        other = 1 - (pair & 1)
        shard_line = (own_shard >> 1 if other == 0 else own_shard >> 4) & 7
        wait_arrived(part_got.at[pair, pl.ds(0, LINE - 1)], part_sem.at[pair])
        total = jnp.zeros((8, LANES), jnp.float32)
        for line in range(LINE):
            value = part_got[pair, line]
            total += jnp.where(parity(shard_line & line) != 0, -value, value)
        picked[my_col, pair // 2, (pair & 1) * 8 : (pair & 1) * 8 + 8, :] = (
            total * own_mask
        )
        if pair & 1:
            for step in (2, 1, 3):
                send(
                    picked.at[my_col, pair // 2],
                    picked.at[my_col, pair // 2],
                    3,
                    picked_sem.at[pair // 2],
                    (me, (my_col + step) & 3),
                )
    wait_left(part_got.at[:, pl.ds(0, LINE - 1)], 2)
    for half in range(2):
        wait_arrived(picked.at[pl.ds(0, 3), half], picked_sem.at[half])
    flat = picked.reshape(COLS * 8, LANES)
    tiles = [flat[pl.ds(t, COLS, stride=8), :] for t in range(SLOT_ROWS)]

    row = iota((COLS, LANES), 0)
    lane = iota((COLS, LANES), 1)
    wide = jnp.zeros((COLS, LANES), jnp.float32)
    for j in range(COLS):
        products = tiles[0] * tiles[0][j : j + 1]
        for tile in tiles[1:]:
            products += tile * tile[j : j + 1]
        column = jnp.sum(products, axis=1, keepdims=True)
        wide = jnp.where(lane == (row & 7) * COLS + j, column, wide)
    wide = wide * (1.0 / (SAMPLE_ROWS * LANES))
    grams[me] = jnp.concatenate(
        [
            jnp.sum(wide[:8], axis=0, keepdims=True),
            jnp.sum(wide[8:], axis=0, keepdims=True),
        ],
        axis=0,
    )

    for target in START_ORDER:

        @pl.when(me != target)
        def _(target=target):
            send(grams.at[me], grams.at[me], 4, gram_sem.at[0], (target, my_col))

    wait_left(picked.at[pl.ds(0, 3)], 3)
    wait_arrived(grams.at[pl.ds(0, SHARDS - 1)], gram_sem.at[0])
    gram = jnp.sum(grams[...], axis=0)

    rows = jnp.concatenate(
        [jnp.broadcast_to(gram[i : i + 1], (8, LANES)) for i in range(2)], axis=0
    )
    rows = jnp.take_along_axis(rows, ((row & 7) * 16 + lane) & (LANES - 1), axis=1)
    columns = [
        jnp.take_along_axis(rows, jnp.full_like(lane, j), axis=1) for j in range(COLS)
    ]
    values = [flat[8 * j : 8 * j + 8, :] for j in range(COLS)]
    upper = jnp.zeros((COLS, LANES), jnp.float32)
    roots = jnp.zeros((COLS, LANES), jnp.float32)
    for j in range(COLS):
        pivot = columns[j][j : j + 1]
        share = jnp.where(row > j, columns[j] * (1.0 / pivot), 0.0)
        for k in range(j + 1, COLS):
            columns[k] -= share * columns[k][j : j + 1]
            values[k] -= share[k : k + 1] * values[j]
        root = 1.0 / jnp.sqrt(pivot)
        solved[j] = values[j] * root
        roots = jnp.where(row == j, root, roots)
        upper = jnp.where((lane == j) & (row <= j), columns[j], upper)
    factor[...] = (upper * roots)[:, :COLS]
    for column in range(WIDTH):
        own = solved[my_col * WIDTH + column]
        for t in range(SLOT_ROWS):
            normalized[column : column + 1, t * LANES : (t + 1) * LANES] = own[t : t + 1]
    wait_left(grams.at[pl.ds(0, SHARDS - 1)], 4)


def local(panel, signs, samples):
    panel = panel.reshape(WIDTH, 2 * ORDER, LANES).transpose(1, 0, 2)
    panel = panel.reshape(2 * ORDER * WIDTH, LANES)
    signs = signs.reshape(2 * ORDER, LANES)
    samples = samples.reshape(SAMPLE_ROWS, LANES)
    f32, i32, dma = jnp.float32, jnp.int32, pltpu.SemaphoreType.DMA
    factor, normalized = pl.pallas_call(
        kernel,
        out_shape=(
            jax.ShapeDtypeStruct((COLS, COLS), f32),
            jax.ShapeDtypeStruct((WIDTH, CAP), f32),
        ),
        in_specs=[pl.BlockSpec(memory_space=pltpu.HBM)] * 3,
        out_specs=[pl.BlockSpec(memory_space=pltpu.VMEM)] * 2,
        scratch_shapes=[
            pltpu.VMEM((2 * ORDER * WIDTH, LANES), f32),
            pltpu.VMEM((2 * ORDER, LANES), i32),
            pltpu.VMEM((SAMPLE_ROWS, LANES), i32),
            pltpu.VMEM((4, 16, 16, ORDER), f32),
            pltpu.VMEM((4, 16, 16, ORDER), f32),
            pltpu.VMEM((8, LANES), i32),
            pltpu.VMEM((8, LANES), f32),
            pltpu.VMEM((2, LINE, 8, LANES), i32),
            pltpu.VMEM((2, 2, SLOT_ROWS, 8, LANES), i32),
            pltpu.VMEM((4, LINE, 8, LANES), f32),
            pltpu.VMEM((4, LINE, 8, LANES), f32),
            pltpu.VMEM((4, 2, 16, LANES), f32),
            pltpu.VMEM((SHARDS, 2, LANES), f32),
            pltpu.VMEM((COLS, 8, LANES), f32),
            dma((3,)),
            dma((5,)),
            dma((2,)),
            dma((6,)),
            dma((4,)),
            dma((2,)),
            dma((1,)),
        ],
        compiler_params=pltpu.CompilerParams(
            collective_id=0, has_side_effects=True, vmem_limit_bytes=55100 * 1024
        ),
    )(panel, signs, samples)
    return factor, normalized


def solution(mesh):
    return jax.shard_map(
        local,
        mesh=mesh,
        in_specs=(P("cols", "rows"), P("rows"), P()),
        out_specs=(P(), P("cols", "rows")),
        check_vma=False,
    )
```

```python
import math

import jax
import jax.numpy as jnp
from jax import lax
from jax.experimental import pallas as pl
from jax.experimental.pallas import tpu as pltpu
from jax.sharding import PartitionSpec as P

LINE = 8
BLK = 512
LANES = 128
SLOT_ROWS = 7
CAP = SLOT_ROWS * LANES
WIDTH = 4
ORDER = 256
SHARDS = 128
LOCAL = ORDER * ORDER
SAMPLE_ROWS = 512
COLS = 16
MESH = pl.DeviceIdType.MESH
HIGHEST = lax.Precision.HIGHEST
DISTANCES = (4, 3, 5, 2, 6, 1, 7)
START_ORDER = sorted(
    range(SHARDS),
    key=lambda at: 1.15 * ((at >> 1) & 7) + 0.9 * min(at >> 4, 8 - (at >> 4)),
)


def iota(shape, axis):
    return lax.broadcasted_iota(jnp.int32, shape, axis)


def parity(value):
    value = value ^ (value >> 4)
    value = value ^ (value >> 2)
    value = value ^ (value >> 1)
    return value & 1


def hadamard_rows(rows):
    odd = parity(rows & iota((ORDER, ORDER), 1))
    return (1 - 2 * odd).astype(jnp.float32).astype(jnp.bfloat16)


def line_rows(half):
    place = iota((ORDER, ORDER), 0)
    line, core, other, part = place >> 5, (place >> 4) & 1, (place >> 1) & 7, place & 1
    if half == 0:
        return other * 32 + line * 4 + core * 2 + part
    return line * 32 + other * 4 + core * 2 + part


def split(values):
    high = values.astype(jnp.bfloat16)
    low = (values - high.astype(jnp.float32)).astype(jnp.bfloat16)
    return high, low


def dot(a, b):
    return jnp.dot(a, b, preferred_element_type=jnp.float32)


def slot_list(samples, device):
    turned = jnp.transpose(samples)
    pieces = [turned & 255, (turned >> 8) & 255, turned >> 16]
    pieces = [p.astype(jnp.float32).astype(jnp.bfloat16) for p in pieces]
    last = samples[:, LANES - 1 :].astype(jnp.float32)
    lane = iota((1, 2 * SHARDS), 1)
    edge = (lane & (SHARDS - 1)) * LOCAL + device * BLK + (lane >> 7) * BLK
    edge = edge.astype(jnp.float32)
    before = jnp.sum((last < edge).astype(jnp.float32), axis=0, keepdims=True)
    row_id = iota((SAMPLE_ROWS, 1), 0).astype(jnp.float32)
    hot = (row_id == before).astype(jnp.float32).astype(jnp.bfloat16)
    rows = dot(jnp.concatenate(pieces, axis=0), hot)
    rows = rows[:LANES] + 256.0 * rows[LANES : 2 * LANES] + 65536.0 * rows[2 * LANES :]
    inside = jnp.sum((rows < edge).astype(jnp.float32), axis=0, keepdims=True)
    whole = jnp.float32(SAMPLE_ROWS * LANES)
    place = jnp.where(before >= SAMPLE_ROWS, whole, before * LANES + inside)
    first = place[:, :SHARDS]
    count = place[:, SHARDS:] - first
    square_row, square_col = iota((SHARDS, SHARDS), 0), iota((SHARDS, SHARDS), 1)
    first_col = jnp.sum(
        jnp.where(square_row == square_col, first, 0.0), axis=1, keepdims=True
    )
    start_col = jnp.sum(
        jnp.where(square_col < square_row, count, 0.0), axis=1, keepdims=True
    )
    end_col = jnp.sum(
        jnp.where(square_col <= square_row, count, 0.0), axis=1, keepdims=True
    )
    slot = iota((1, CAP), 1).astype(jnp.float32)
    owner = jnp.sum((slot >= end_col).astype(jnp.float32), axis=0, keepdims=True)
    shard_id = iota((SHARDS, 1), 0).astype(jnp.float32)
    shift = jnp.sum(
        jnp.where(shard_id == owner, first_col - start_col, 0.0), axis=0, keepdims=True
    )
    index = slot + shift
    row = jnp.floor(index * (1.0 / LANES))
    column = index - row * LANES
    hot = (row_id == row).astype(jnp.float32).astype(jnp.bfloat16)
    bit = ((turned >> 8) & 1).astype(jnp.float32).astype(jnp.bfloat16)
    found = dot(jnp.concatenate([pieces[0], bit], axis=0), hot)
    found = found[:LANES] + 256.0 * found[LANES:]
    lane_id = iota((LANES, 1), 0).astype(jnp.float32)
    position = jnp.sum(
        jnp.where(lane_id == column, found, 0.0), axis=0, keepdims=True
    )
    used = owner < SHARDS
    code = jnp.where(used, owner * BLK + position, 0.0)
    return code.astype(jnp.int32), used.astype(jnp.float32)


def kernel(
    panel,
    signs,
    samples,
    factor,
    normalized,
    panel_v,
    signs_v,
    samples_v,
    sent,
    got,
    own_list,
    own_used,
    lists,
    codes,
    part_sent,
    part_got,
    picked,
    grams,
    solved,
    local_sem,
    out_sem,
    list_sem,
    block_sem,
    part_sem,
    picked_sem,
    gram_sem,
):
    scale = 1.0 / math.sqrt(LOCAL * SHARDS)
    me = lax.axis_index("rows")
    my_col = lax.axis_index("cols")
    my_y, my_z, my_core = me >> 4, (me >> 1) & 7, me & 1
    my_lines = (my_z, my_y)
    my_sources = [my_lines[half] * 2 + my_core for half in range(2)]

    def device(half, line, core):
        if half == 0:
            return (my_y * 16 + line * 2 + core, my_col)
        return (line * 16 + my_z * 2 + core, my_col)

    def on_line(half, distance):
        return (my_lines[half] + distance) & 7

    def send(src, dst, out, arrived, target):
        pltpu.make_async_remote_copy(
            src_ref=src,
            dst_ref=dst,
            send_sem=out_sem.at[out],
            recv_sem=arrived,
            device_id=target,
            device_id_type=MESH,
        ).start()

    def wait_arrived(like, arrived):
        pltpu.make_async_copy(like, like, arrived).wait()

    def wait_left(like, out):
        pltpu.make_async_copy(like, like, out_sem.at[out]).wait()

    barrier = pltpu.get_barrier_semaphore()

    def greet(target):
        pl.semaphore_signal(barrier, inc=1, device_id=target, device_id_type=MESH)

    for distance in DISTANCES:
        for half in range(2):
            for flip in range(2):
                greet(device(half, on_line(half, distance), my_core ^ flip))
    for step in range(1, 4):
        greet((me, (my_col + step) & 3))
    greet(device(0, my_z, 1 - my_core))

    loads = [
        pltpu.make_async_copy(panel, panel_v, local_sem.at[2]),
        pltpu.make_async_copy(signs, signs_v, local_sem.at[1]),
        pltpu.make_async_copy(samples, samples_v, local_sem.at[0]),
    ]
    for load in loads:
        load.start()

    inner = hadamard_rows(iota((ORDER, ORDER), 0))
    outer = []
    for half in range(2):
        matrix = hadamard_rows(line_rows(half))
        outer.append(jnp.concatenate([matrix, matrix], axis=1))

    loads[1].wait()
    loads[0].wait()
    flip_signs = jnp.concatenate(
        [signs_v[pl.ds(j, ORDER, stride=2), :] for j in range(2)], axis=1
    )
    flip_signs = flip_signs.astype(jnp.float32) * scale

    def transform(pair):
        half = pair & 1
        values = jnp.concatenate(
            [panel_v[pl.ds(4 * j + pair, ORDER, stride=8), :] for j in range(2)],
            axis=1,
        )
        high, low = split(values * flip_signs)
        values = dot(jnp.concatenate([high, low], axis=0), inner)
        values = values[:ORDER] + values[ORDER:]
        high, low = split(values)
        values = dot(outer[half], jnp.concatenate([high, low], axis=0))
        sent[pair] = values.reshape(16, 16, ORDER)
        got[pair, my_sources[half]] = sent[pair, my_sources[half]]

    def send_block(pair, half, line, core, rows, arrived):
        send(
            sent.at[pair, line * 2 + core, rows],
            got.at[pair, my_sources[half], rows],
            1,
            block_sem.at[arrived],
            device(half, line, core),
        )

    def send_blocks(first, rows, arrived):
        for distance in DISTANCES:
            for half in range(2):
                for flip in range(2):
                    line = on_line(half, distance)
                    send_block(
                        first + half, half, line, my_core ^ flip, rows, arrived + half
                    )
        for half in range(2):
            send_block(
                first + half, half, my_lines[half], 1 - my_core, rows, arrived + half
            )

    transform(0)
    transform(1)
    pl.semaphore_wait(barrier, 32)
    send_blocks(0, pl.ds(0, 16), 0)
    transform(2)
    transform(3)

    loads[2].wait()
    code, used = slot_list(samples_v[...], me)
    for t in range(SLOT_ROWS):
        own_list[t : t + 1, :] = code[:, t * LANES : (t + 1) * LANES]
        own_used[t : t + 1, :] = used[:, t * LANES : (t + 1) * LANES]
    own_list[SLOT_ROWS:, :] = jnp.zeros((1, LANES), jnp.int32)
    own_used[SLOT_ROWS:, :] = jnp.zeros((1, LANES), jnp.float32)
    for half in range(2):
        lists[half, my_lines[half]] = own_list[...]
        for distance in DISTANCES:
            line = on_line(half, distance)
            send(
                own_list,
                lists.at[half, my_lines[half]],
                0,
                list_sem.at[half],
                device(half, line, my_core),
            )
    for group in range(2):
        send_blocks(2, pl.ds(8 * group, 8), 2 + 2 * group)

    spread = iota((8, LANES), 0) >> 1
    for half in range(2):
        wait_arrived(lists.at[half, pl.ds(0, LINE - 1)], list_sem.at[half])
        flat = lists.at[half].reshape(64, LANES)
        for t in range(SLOT_ROWS):
            rows = flat[pl.ds(t, 8, stride=8), :]
            for group in range(2):
                codes[1 - half, group, t] = jnp.take_along_axis(
                    rows, spread + 4 * group, axis=0, mode="promise_in_bounds")

    odd_row = iota((8, LANES), 0) & 1
    for pair in range(4):
        for line in range(LINE):
            part_sent[pair, line, SLOT_ROWS:, :] = jnp.zeros((1, LANES), jnp.float32)

    def sample(pair, groups):
        half = pair & 1

        def add_sources(t, carry):
            for group in groups:
                code = codes[half, group, t]
                lane = code & (LANES - 1)
                right = (code & LANES) != 0
                bits = (9, 10, 11, 12) if half == 0 else (9, 13, 14, 15)
                signs = [jnp.where((code & (1 << b)) != 0, -1.0, 1.0) for b in bits]

                def total(first, level):
                    if level == 0:
                        table = got[pair, first, group * 8 : group * 8 + 8, :]
                        a = jnp.take_along_axis(table[:, :LANES], lane, axis=1, mode="promise_in_bounds")
                        b = jnp.take_along_axis(table[:, LANES:], lane, axis=1, mode="promise_in_bounds")
                        return jnp.where(right, b, a)
                    upper = total(first + (1 << (level - 1)), level - 1)
                    return total(first, level - 1) + signs[level - 1] * upper

                value = total(0, 4)
                value = jnp.where(((code >> 8) & 1) == odd_row, value, 0.0)
                value = value + pltpu.roll(value, 7, 0)
                for line in range(4):
                    part_sent[pair, group * 4 + line, pl.ds(t, 1), :] = value[
                        2 * line : 2 * line + 1
                    ]
            return carry

        lax.fori_loop(0, SLOT_ROWS, add_sources, 0, unroll=True)

    def send_sums(pair, line):
        other = 1 - (pair & 1)
        send(
            part_sent.at[pair, line],
            part_got.at[pair, my_lines[other]],
            2,
            part_sem.at[pair],
            device(other, line, my_core),
        )

    for pair in range(2):
        other = 1 - pair
        wait_arrived(got.at[pair, pl.ds(0, 15)], block_sem.at[pair])
        sample(pair, (0, 1))
        for distance in DISTANCES:
            send_sums(pair, on_line(other, distance))
        part_got[pair, my_lines[other]] = part_sent[pair, my_lines[other]]
    for group in range(2):
        for pair in range(2, 4):
            other = 1 - (pair & 1)
            wait_arrived(
                got.at[pair, pl.ds(0, 15), pl.ds(0, 8)], block_sem.at[pair + 2 * group]
            )
            sample(pair, (group,))
            for line in range(4 * group, 4 * group + 4):

                @pl.when(line != my_lines[other])
                def _(pair=pair, line=line):
                    send_sums(pair, line)

    for pair in range(2, 4):
        other = 1 - (pair & 1)
        part_got[pair, my_lines[other]] = part_sent[pair, my_lines[other]]

    wait_left(lists.at[:, pl.ds(0, LINE - 1)], 0)
    wait_left(got.at[:, pl.ds(0, 15)], 1)

    own_shard = own_list[...] >> 9
    own_mask = own_used[...]
    for pair in range(4):
        other = 1 - (pair & 1)
        shard_line = (own_shard >> 1 if other == 0 else own_shard >> 4) & 7
        wait_arrived(part_got.at[pair, pl.ds(0, LINE - 1)], part_sem.at[pair])
        signs = [jnp.where((shard_line & (1 << b)) != 0, -1.0, 1.0) for b in range(3)]
        parts = [part_got[pair, line] for line in range(LINE)]
        for sign in signs:
            parts = [a + sign * b for a, b in zip(parts[::2], parts[1::2])]
        total = parts[0]
        picked[my_col, pair // 2, (pair & 1) * 8 : (pair & 1) * 8 + 8, :] = (
            total * own_mask
        )
        if pair & 1:
            for step in (2, 1, 3):
                send(
                    picked.at[my_col, pair // 2],
                    picked.at[my_col, pair // 2],
                    3,
                    picked_sem.at[pair // 2],
                    (me, (my_col + step) & 3),
                )
    wait_left(part_got.at[:, pl.ds(0, LINE - 1)], 2)
    for half in range(2):
        wait_arrived(picked.at[pl.ds(0, 3), half], picked_sem.at[half])
    flat = picked.reshape(COLS * 8, LANES)
    tiles = [flat[pl.ds(t, COLS, stride=8), :] for t in range(SLOT_ROWS)]

    row = iota((COLS, LANES), 0)
    lane = iota((COLS, LANES), 1)
    wide = jnp.zeros((COLS, LANES), jnp.float32)
    for j in range(COLS):
        products = tiles[0] * tiles[0][j : j + 1]
        for tile in tiles[1:]:
            products += tile * tile[j : j + 1]
        column = jnp.sum(products, axis=1, keepdims=True)
        wide = jnp.where(lane == (row & 7) * COLS + j, column, wide)
    wide = wide * (1.0 / (SAMPLE_ROWS * LANES))
    grams[me] = jnp.concatenate(
        [
            jnp.sum(wide[:8], axis=0, keepdims=True),
            jnp.sum(wide[8:], axis=0, keepdims=True),
        ],
        axis=0,
    )

    for target in START_ORDER:

        @pl.when(me != target)
        def _(target=target):
            send(grams.at[me], grams.at[me], 4, gram_sem.at[0], (target, my_col))

    wait_left(picked.at[pl.ds(0, 3)], 3)
    wait_arrived(grams.at[pl.ds(0, SHARDS - 1)], gram_sem.at[0])
    gram = jnp.sum(grams[...], axis=0)

    rows = jnp.concatenate(
        [jnp.broadcast_to(gram[i : i + 1], (8, LANES)) for i in range(2)], axis=0
    )
    rows = jnp.take_along_axis(rows, ((row & 7) * 16 + lane) & (LANES - 1), axis=1)
    columns = [
        jnp.take_along_axis(rows, jnp.full_like(lane, j), axis=1, mode="promise_in_bounds") for j in range(COLS)
    ]
    values = [flat[8 * j : 8 * j + 8, :] for j in range(COLS)]
    upper = jnp.zeros((COLS, LANES), jnp.float32)
    roots = jnp.zeros((COLS, LANES), jnp.float32)
    for j in range(COLS):
        pivot = columns[j][j : j + 1]
        share = jnp.where(row > j, columns[j] * (1.0 / pivot), 0.0)
        for k in range(j + 1, COLS):
            columns[k] -= share * columns[k][j : j + 1]
            values[k] -= share[k : k + 1] * values[j]
        root = 1.0 / jnp.sqrt(pivot)
        solved[j] = values[j] * root
        roots = jnp.where(row == j, root, roots)
        upper = jnp.where((lane == j) & (row <= j), columns[j], upper)
    factor[...] = (upper * roots)[:, :COLS]
    for column in range(WIDTH):
        own = solved[my_col * WIDTH + column]
        for t in range(SLOT_ROWS):
            normalized[column : column + 1, t * LANES : (t + 1) * LANES] = own[t : t + 1]
    wait_left(grams.at[pl.ds(0, SHARDS - 1)], 4)


def local(panel, signs, samples):
    panel = panel.reshape(WIDTH, 2 * ORDER, LANES).transpose(1, 0, 2)
    panel = panel.reshape(2 * ORDER * WIDTH, LANES)
    signs = signs.reshape(2 * ORDER, LANES)
    samples = samples.reshape(SAMPLE_ROWS, LANES)
    f32, i32, dma = jnp.float32, jnp.int32, pltpu.SemaphoreType.DMA
    factor, normalized = pl.pallas_call(
        kernel,
        out_shape=(
            jax.ShapeDtypeStruct((COLS, COLS), f32),
            jax.ShapeDtypeStruct((WIDTH, CAP), f32),
        ),
        in_specs=[pl.BlockSpec(memory_space=pltpu.HBM)] * 3,
        out_specs=[pl.BlockSpec(memory_space=pltpu.VMEM)] * 2,
        scratch_shapes=[
            pltpu.VMEM((2 * ORDER * WIDTH, LANES), f32),
            pltpu.VMEM((2 * ORDER, LANES), i32),
            pltpu.VMEM((SAMPLE_ROWS, LANES), i32),
            pltpu.VMEM((4, 16, 16, ORDER), f32),
            pltpu.VMEM((4, 16, 16, ORDER), f32),
            pltpu.VMEM((8, LANES), i32),
            pltpu.VMEM((8, LANES), f32),
            pltpu.VMEM((2, LINE, 8, LANES), i32),
            pltpu.VMEM((2, 2, SLOT_ROWS, 8, LANES), i32),
            pltpu.VMEM((4, LINE, 8, LANES), f32),
            pltpu.VMEM((4, LINE, 8, LANES), f32),
            pltpu.VMEM((4, 2, 16, LANES), f32),
            pltpu.VMEM((SHARDS, 2, LANES), f32),
            pltpu.VMEM((COLS, 8, LANES), f32),
            dma((3,)),
            dma((5,)),
            dma((2,)),
            dma((6,)),
            dma((4,)),
            dma((2,)),
            dma((1,)),
        ],
        compiler_params=pltpu.CompilerParams(
            collective_id=0, has_side_effects=True, vmem_limit_bytes=55100 * 1024
        ),
    )(panel, signs, samples)
    return factor, normalized


def solution(mesh):
    return jax.shard_map(
        local,
        mesh=mesh,
        in_specs=(P("cols", "rows"), P("rows"), P()),
        out_specs=(P(), P("cols", "rows")),
        check_vma=False,
    )
```
